256 devices in a mesh: dp: 8 (over x, core), ctx: 32 (over z, y).
Axes of the slice: x: 4, y: 4, z: 8, core: 2. Of those that a mesh axis runs over, the one named last changes fastest.
Arguments:
- injected_early: bfloat16 [8, 640, 4608], P('dp', 'ctx'), may hold values from -6 to 6
- injected_middle: bfloat16 [8, 640, 4608], P('dp', 'ctx'), may hold values from -6 to 6
- injected_late: bfloat16 [8, 640, 4608], P('dp', 'ctx'), may hold values from -6 to 6
- slot_source: int32 [8, 1024], P('dp', 'ctx'), may hold values from -1 to 639, as said below
- saved_early: bfloat16 [8, 4096, 1152], P('dp', 'ctx'), may hold values from -0.023925781 to 0.023925781
- projection_early: bfloat16 [1152, 1152], P('dp'), may hold values from -0.1875 to 0.1875
- projection_middle: bfloat16 [1152, 1152], P('dp'), may hold values from -0.1875 to 0.1875
- projection_late: bfloat16 [1152, 1152], P('dp'), may hold values from -0.1875 to 0.1875
Outputs:
- context_early: bfloat16 [8, 4096, 1152], P('dp', 'ctx')
- context_middle: bfloat16 [8, 4096, 1152], P('dp', 'ctx')
- context_late: bfloat16 [8, 4096, 1152], P('dp', 'ctx')
- stream_gradient: bfloat16 [8, 4096, 1152], P('dp', 'ctx')
- projection_gradient: float32 [1152, 1152], P('ctx', 'dp')
The draws below stay inside these ranges and needn't reach their ends.
Inputs may be any that keep to these rules, and one draw needn't show every extreme that they name: `slot_source`: in each group the entries other than -1 name every visual token 0 to 639 once. Token q lies on context device q // 20; slot e lies on device e // 32. Each aligned block of 32 slots holds one image: its tokens, in order, fill the block's first slots and the rest are -1. Of the tokens of one device at most 1 fill slots of one device, and in every group one device receives exactly 1 from every device.
All inputs are finite; a program needn't handle non-finite values.
Results may differ from the reference program's by a relative error of at most 0.0051.
Values may be sent and summed in bfloat16 or wider, within the bound.
No kernel may reach another device: no remote copies, remote signals or barrier semaphores. Data moves between devices by JAX's collectives and lax.ppermute only.
A program may use at most 128 MiB of HBM per device.

```python
import jax
import jax.numpy as jnp
from jax import lax

VIT_D = 1152
MERGE = 4
BLOCK = 32
EBLK = 1
MERGED_D = 4608
VIS_DEV = 20
GROUPS = 8
CTX_DEVS = 32
VIS_TOTAL = 640
SLOTS = 1024
PATCHES = 4096


def group_slots(key):
    key_owner, key_cells, key_blocks, key_order = jax.random.split(key, 4)
    images = CTX_DEVS * EBLK
    others = images - EBLK
    full_owner = jax.random.randint(key_owner, (), 0, CTX_DEVS).astype(jnp.int32)
    extras = VIS_TOTAL - EBLK * BLOCK - others
    shuffled = jax.random.permutation(key_cells, others * (BLOCK - 1)).astype(jnp.int32)
    chosen = (shuffled < extras).astype(jnp.int32).reshape(others, BLOCK - 1)
    lengths = jnp.concatenate([jnp.full((EBLK,), BLOCK, jnp.int32), 1 + jnp.sum(chosen, axis=1).astype(jnp.int32)])
    rest_ids = jnp.arange(others, dtype=jnp.int32)
    rest_ids = rest_ids + EBLK * (rest_ids >= full_owner * EBLK).astype(jnp.int32)
    rest_ids = rest_ids[jax.random.permutation(key_blocks, others).astype(jnp.int32)]
    full_ids = full_owner * EBLK + jax.random.permutation(key_order, EBLK).astype(jnp.int32)
    block_ids = jnp.concatenate([full_ids, rest_ids])
    starts = jnp.cumsum(lengths).astype(jnp.int32) - lengths
    position = jnp.arange(VIS_TOTAL, dtype=jnp.int32)
    image_index = jnp.sum((starts[None, :] <= position[:, None]).astype(jnp.int32), axis=1) - 1
    offset = position - starts[image_index]
    target = block_ids[image_index] * BLOCK + offset
    source = position % CTX_DEVS * VIS_DEV + position // CTX_DEVS
    return jnp.full((SLOTS,), -1, jnp.int32).at[target].set(source)


def draw_slot_source(key, part):
    key = jax.random.fold_in(key, 7)
    return jax.vmap(group_slots)(jax.random.split(key, GROUPS))


def spiked(array, stream_key, source, target, blocks, factor):
    def block_of(axis_at):
        return (jnp.arange(array.shape[axis_at]) // (array.shape[axis_at] // blocks)).reshape((-1,) + (1,) * (array.ndim - 1 - axis_at))

    first = jax.random.permutation(stream_key, blocks)[block_of(target)]
    other_side = (block_of(target) + blocks // 2) % blocks
    return jnp.where((block_of(source) == first) | (block_of(source) == other_side), factor * array, array)


def levels(own_key, extent, shards, low, high):
    loudness = 1.0
    for dim, shards_of in shards:
        steps = jax.random.uniform(jax.random.fold_in(jax.random.fold_in(own_key, 6), dim), (shards_of,), jnp.float32, low / len(shards), high / len(shards))
        loudness = loudness * jnp.repeat(jnp.exp(steps), extent[dim] // shards_of).reshape((-1,) + (1,) * (len(extent) - 1 - dim))
    return loudness


def bell_draw(stream_key, shape, scale, most, pieces=(), kind=jnp.bfloat16):
    level = levels(stream_key, shape, pieces, -0.22, 0.18) if pieces else 1.0
    values = jax.random.normal(stream_key, shape, jnp.float32) * scale * level
    return jnp.minimum(jnp.maximum(values, -most), most).astype(kind)


def bell_draw_with(key, extent, width, most, pieces, heavy, kind=jnp.bfloat16):
    values = width * jax.random.normal(key, extent, jnp.float32)
    if pieces:
        values = values * levels(key, extent, pieces, -0.22, 0.18)
    return jnp.clip(spiked(values, jax.random.fold_in(key, 3), *heavy), -most, most).astype(kind)


def setup_inputs(seed: int = 0) -> dict:
    key_of = jax.random.split(jax.random.key(seed), 9)
    injected_early = bell_draw(key_of[0], (GROUPS, VIS_TOTAL, MERGED_D), 1.0, 6.0, ((0, 8), (1, 32)))
    injected_middle = bell_draw(key_of[1], (GROUPS, VIS_TOTAL, MERGED_D), 1.0, 6.0, ((0, 8), (1, 32)))
    injected_late = bell_draw(key_of[2], (GROUPS, VIS_TOTAL, MERGED_D), 1.0, 6.0, ((0, 8), (1, 32)))
    slot_source = draw_slot_source(jax.random.fold_in(key_of[8], 71), 0)
    saved_early = bell_draw_with(key_of[4], (GROUPS, PATCHES, VIT_D), 0.004, 0.023925781, ((0, 8), (1, 32)), (1, 2, 32, 2.75))
    projection_early = bell_draw(key_of[5], (VIT_D, VIT_D), VIT_D ** -0.5, 0.1875, ((0, 8),))
    projection_middle = bell_draw(key_of[6], (VIT_D, VIT_D), VIT_D ** -0.5, 0.1875, ((0, 8),))
    projection_late = bell_draw(key_of[7], (VIT_D, VIT_D), VIT_D ** -0.5, 0.1875, ((0, 8),))
    return {"injected_early": injected_early, "injected_middle": injected_middle, "injected_late": injected_late, "slot_source": slot_source, "saved_early": saved_early, "projection_early": projection_early, "projection_middle": projection_middle, "projection_late": projection_late}


def placed_rows(rows, sources):
    filled = sources >= 0
    taken = jnp.take(rows, jnp.maximum(sources, 0).astype(jnp.int32), axis=0)
    taken = jnp.where(filled[:, None], taken, jnp.zeros_like(taken))
    return taken.reshape(SLOTS * MERGE, VIT_D)


def context_of(rounded, projection):
    flat = rounded.reshape(GROUPS * PATCHES, VIT_D)
    result = jnp.dot(flat, projection.T, preferred_element_type=jnp.float32)
    return result.astype(jnp.bfloat16).reshape(GROUPS, PATCHES, VIT_D)


def weight_of(saved, rounded):
    return jnp.dot(saved.reshape(GROUPS * PATCHES, VIT_D).T, rounded.reshape(GROUPS * PATCHES, VIT_D), preferred_element_type=jnp.float32)


def reference(injected_early, injected_middle, injected_late, slot_source, saved_early, projection_early, projection_middle, projection_late):
    def per_group(items):
        early_rows, middle_rows, late_rows, sources = items
        down_late = placed_rows(late_rows, sources).astype(jnp.float32)
        down_middle = down_late + placed_rows(middle_rows, sources).astype(jnp.float32)
        down_early = down_middle + placed_rows(early_rows, sources).astype(jnp.float32)
        return (down_late.astype(jnp.bfloat16), down_middle.astype(jnp.bfloat16), down_early.astype(jnp.bfloat16))

    rounded_late, rounded_middle, rounded_early = lax.map(per_group, (injected_early, injected_middle, injected_late, slot_source))
    context_early = context_of(rounded_early, projection_early)
    context_middle = context_of(rounded_middle, projection_middle)
    context_late = context_of(rounded_late, projection_late)
    projection_gradient = weight_of(saved_early, rounded_early)
    return (context_early, context_middle, context_late, rounded_early, projection_gradient)
```

```python
import jax
import jax.numpy as jnp
from jax import lax
from jax.experimental import pallas as pl
from jax.experimental.pallas import tpu as pltpu
from jax.sharding import Mesh, PartitionSpec as P

DP = ("x", "core")
CTX = ("z", "y")
BF16 = jnp.bfloat16
F32 = jnp.float32


def turn(size, step):
    return [(i, (i + step) % size) for i in range(size)]


def select(rows, table):
    return jnp.dot(table.astype(BF16), rows, preferred_element_type=F32).astype(BF16)


def context_kernel(core_ref, rounded_ref, own_ref, other_ref, out_ref, weight, sem):
    core = core_ref[0]
    xs, rows = own_ref.shape[0], own_ref.shape[2]
    matrices = own_ref.shape[1]
    copies = []
    for m in range(matrices):
        for x in range(xs):
            for ref, c in ((own_ref, core), (other_ref, 1 - core)):
                at = pl.multiple_of((2 * x + c) * rows, 16)
                copies.append(
                    pltpu.make_async_copy(ref.at[x, m], weight.at[m, pl.ds(at, rows)], sem.at[m])
                )
    for copy in copies:
        copy.start()
    per = len(copies) // matrices
    for m in range(matrices):
        for copy in copies[m * per : (m + 1) * per]:
            copy.wait()
        out_ref[m] = lax.dot_general(
            rounded_ref[m], weight[m], (((1,), (1,)), ((), ())), preferred_element_type=F32
        ).astype(BF16)


def contexts(core, rounded, own, other):
    matrices, rows, width = rounded.shape
    return pl.pallas_call(
        context_kernel,
        out_shape=jax.ShapeDtypeStruct((matrices, rows, width), BF16),
        in_specs=[
            pl.BlockSpec(memory_space=pltpu.SMEM),
            pl.BlockSpec(memory_space=pltpu.VMEM),
            pl.BlockSpec(memory_space=pl.ANY),
            pl.BlockSpec(memory_space=pl.ANY),
        ],
        out_specs=pl.BlockSpec(memory_space=pltpu.VMEM),
        scratch_shapes=[
            pltpu.VMEM((matrices, width, width), BF16),
            pltpu.SemaphoreType.DMA((matrices,)),
        ],
        compiler_params=pltpu.CompilerParams(vmem_limit_bytes=32 << 20),
        cost_estimate=pl.CostEstimate(
            flops=2 * matrices * rows * width * width,
            bytes_accessed=2 * matrices * width * width,
            transcendentals=0,
        ),
    )(core, rounded, own, other)


def local(
    injected_early,
    injected_middle,
    injected_late,
    slot_source,
    saved_early,
    projection_early,
    projection_middle,
    projection_late,
):
    devices = lax.axis_size(CTX)
    xs, cores = lax.axis_size("x"), lax.axis_size("core")
    core = lax.axis_index("core")
    tokens, merged = injected_early.shape[1:]
    slots = slot_source.shape[1]
    patches, width = saved_early.shape[1:]
    merge = merged // width
    share = width // (xs * cores)

    stacked = jnp.stack([projection_early, projection_middle, projection_late])
    own = lax.all_gather(stacked, "x", axis=0)
    other = lax.ppermute(own, "core", turn(cores, 1))

    late = injected_late[0].reshape(tokens * merge, width)
    middle32 = late.astype(F32) + injected_middle[0].reshape(tokens * merge, width).astype(F32)
    early32 = middle32 + injected_early[0].reshape(tokens * merge, width).astype(F32)
    middle, early = middle32.astype(BF16), early32.astype(BF16)

    source = slot_source[0]
    filled = source >= 0
    sender = jnp.where(filled, source // tokens, -1)
    place = jnp.where(filled, source % tokens, 0)
    patch = jnp.arange(merge * slots, dtype=jnp.int32)
    sender_patch = jnp.repeat(sender, merge)
    by_sender = (sender_patch[None, :] == patch[:, None] // merge) & (
        patch[None, :] % merge == patch[:, None] % merge
    )
    outgoing = select(saved_early[0], by_sender)
    device = jnp.arange(devices, dtype=jnp.int32)
    wanted = jnp.sum(
        jnp.where(sender[None, :] == device[:, None], place[None, :] + 1, 0), axis=1
    )
    tag = jnp.broadcast_to(wanted[:, None, None], (devices, merge, 128)).astype(BF16)
    message = jnp.concatenate([outgoing.reshape(devices, merge, width), tag], axis=2)
    arrived = lax.all_to_all(message, CTX, 0, 0, tiled=True)
    asked = arrived[:, 0, width].astype(jnp.int32) - 1
    asked_patch = jnp.repeat(asked, merge)
    token_patch = jnp.arange(merge * tokens, dtype=jnp.int32)
    by_token = (asked_patch[None, :] == token_patch[:, None] // merge) & (
        patch[None, :] % merge == token_patch[:, None] % merge
    )
    saved_rows = select(arrived[:, :, :width].reshape(devices * merge, width), by_token)

    rows = jnp.concatenate([early, middle, late], axis=1)
    packed = select(rows, by_token.T).reshape(devices, merge, 3 * width)
    landed = lax.all_to_all(packed, CTX, 0, 0, tiled=True).reshape(devices * merge, 3 * width)
    placed = select(landed, by_sender.T)
    rounded = jnp.stack([placed[:, i * width : (i + 1) * width] for i in range(3)])

    pieces = early.reshape(tokens * merge, xs * cores, share).swapaxes(0, 1)
    columns = lax.all_to_all(pieces, DP, 0, 0, tiled=True).reshape(-1, share)
    gathered = lax.all_gather(saved_rows, DP, axis=0, tiled=True)
    partial = lax.dot_general(
        gathered, columns, (((0,), (0,)), ((), ())), preferred_element_type=F32
    ).astype(BF16)
    terms = lax.all_to_all(
        partial.reshape(devices, width // devices * share), CTX, 0, 0, tiled=True
    )
    weights = jnp.sum(terms.astype(F32), axis=0).reshape(width // devices, share)

    out = contexts(jnp.full((1,), core, jnp.int32), rounded, own, other)
    return out[0][None], out[1][None], out[2][None], rounded[0][None], weights


def solution(mesh):
    shape = mesh.shape
    fine = Mesh(mesh.devices.reshape(shape["dp"] // 2, 2, -1, 4), ("x", "core", "z", "y"))
    rows = P(DP, CTX, None)
    return jax.shard_map(
        local,
        mesh=fine,
        in_specs=(rows, rows, rows, P(DP, CTX), rows, P(DP, None), P(DP, None), P(DP, None)),
        out_specs=(rows, rows, rows, rows, P(CTX, DP)),
        check_vma=False,
    )
```

```python
import jax
import jax.numpy as jnp
from jax import lax
from jax.experimental import pallas as pl
from jax.experimental.pallas import tpu as pltpu
from jax.sharding import Mesh, PartitionSpec as P

DP = ("x", "core")
CTX = ("z", "y")
BF16 = jnp.bfloat16
F32 = jnp.float32
VMEM = pl.BlockSpec(memory_space=pltpu.VMEM)
SMEM = pl.BlockSpec(memory_space=pltpu.SMEM)
ANY = pl.BlockSpec(memory_space=pl.ANY)


def over_x(array, step):
    size = lax.axis_size("x")
    return lax.ppermute(array, "x", [(i, (i + step) % size) for i in range(size)])


def over_core(array):
    return lax.ppermute(array, "core", [(0, 1), (1, 0)])


def select(rows, table):
    return jnp.dot(table.astype(BF16), rows, preferred_element_type=F32).astype(BF16)


def context_kernel(shard, cut, at_ref, table_ref, landed_ref, *refs):
    pieces = refs[:10]
    early_out, middle_out, late_out, stream_out, weight, sem = refs[10:]
    x, core = at_ref[0], at_ref[1]
    width = weight.shape[1]
    copies = ([], [], [])

    def put(ref, first, rows, m, inside, of_x, of_core):
        base = pl.multiple_of((2 * of_x + of_core) * shard + inside, 16)
        copies[m].append(
            pltpu.make_async_copy(
                ref.at[pl.ds(first, rows)], weight.at[m, pl.ds(base, rows)], sem.at[m]
            )
        )

    for index, of_core in ((0, core), (5, 1 - core)):
        for k, step in enumerate((0, 3, 1)):
            of_x = lax.rem(x + step, 4)
            for m in range(3):
                put(pieces[index + k], m * shard, shard, m, 0, of_x, of_core)
        of_x = lax.rem(x + 2, 4)
        for ref, start, stop in ((pieces[index + 3], 0, cut), (pieces[index + 4], cut, 3 * shard)):
            for m in range(3):
                low, high = max(start, m * shard), min(stop, (m + 1) * shard)
                if low < high:
                    put(ref, low - start, high - low, m, low - m * shard, of_x, of_core)
    for m in range(3):
        for copy in copies[m]:
            copy.start()
    rounded = jnp.dot(
        table_ref[...], landed_ref[...], preferred_element_type=F32
    ).astype(BF16)
    stream_out[...] = rounded[:, :width]
    for m, out in enumerate((early_out, middle_out, late_out)):
        for copy in copies[m]:
            copy.wait()
        out[...] = lax.dot_general(
            rounded[:, m * width : (m + 1) * width],
            weight[m],
            (((1,), (1,)), ((), ())),
            preferred_element_type=F32,
        ).astype(BF16)


def contexts(at, table, landed, pieces, shard, cut):
    rows, width = table.shape[0], landed.shape[1] // 3
    out = jax.ShapeDtypeStruct((rows, width), BF16)
    return pl.pallas_call(
        lambda *refs: context_kernel(shard, cut, *refs),
        out_shape=(out,) * 4,
        in_specs=[SMEM, VMEM, VMEM] + [ANY] * 10,
        out_specs=(VMEM,) * 4,
        scratch_shapes=[
            pltpu.VMEM((3, width, width), BF16),
            pltpu.SemaphoreType.DMA((3,)),
        ],
        compiler_params=pltpu.CompilerParams(vmem_limit_bytes=32 << 20),
        cost_estimate=pl.CostEstimate(
            flops=6 * rows * width * width, bytes_accessed=6 * width * width, transcendentals=0
        ),
    )(at, table, landed, *pieces)


def gradient_kernel(saved0, saved1, saved2, saved3, keep, give, keep_out, give_out):
    saved = (saved0, saved1, saved2, saved3)

    def product(columns):
        return sum(
            lax.dot_general(
                saved[k][...], columns[k], (((0,), (0,)), ((), ())), preferred_element_type=F32
            )
            for k in range(4)
        )

    give_out[...] = product(give).astype(BF16)
    keep_out[...] = product(keep)


def gradient(saved, keep, give):
    width, share = saved[0].shape[1], keep.shape[2]
    return pl.pallas_call(
        gradient_kernel,
        out_shape=(
            jax.ShapeDtypeStruct((width, share), F32),
            jax.ShapeDtypeStruct((width, share), BF16),
        ),
        in_specs=[VMEM] * 6,
        out_specs=(VMEM,) * 2,
        compiler_params=pltpu.CompilerParams(vmem_limit_bytes=32 << 20),
    )(*saved, keep, give)


def local(
    injected_early,
    injected_middle,
    injected_late,
    slot_source,
    saved_early,
    projection_early,
    projection_middle,
    projection_late,
):
    devices = lax.axis_size(CTX)
    x, core = lax.axis_index("x"), lax.axis_index("core")
    tokens, merged = injected_early.shape[1:]
    slots = slot_source.shape[1]
    width = saved_early.shape[2]
    merge = merged // width
    shard = projection_early.shape[0]
    share = width // 8

    stacked = jnp.concatenate([projection_early, projection_middle, projection_late])
    cut = -(-stacked.shape[0] // 32) * 16
    from_left, from_right = over_x(stacked, 1), over_x(stacked, 3)
    far_left, far_right = over_x(from_left[:cut], 1), over_x(from_right[cut:], 3)
    pieces = (stacked, from_left, from_right, far_left, far_right)
    pieces = pieces + tuple(over_core(piece) for piece in pieces)

    late = injected_late[0].reshape(tokens * merge, width)
    middle32 = late.astype(F32) + injected_middle[0].reshape(tokens * merge, width).astype(F32)
    early32 = middle32 + injected_early[0].reshape(tokens * merge, width).astype(F32)
    middle, early = middle32.astype(BF16), early32.astype(BF16)

    columns = early.reshape(tokens * merge, 4, 2, share).transpose(1, 2, 0, 3)
    columns = jnp.where(core == 0, columns, columns[:, ::-1])
    shares = [
        lax.dynamic_index_in_dim(columns, (x + step) % 4, 0, keepdims=False) for step in range(4)
    ]
    shares = [shares[0]] + [over_x(shares[step], step) for step in (1, 2, 3)]
    keep = jnp.stack([piece[0] for piece in shares])
    give = jnp.stack([piece[1] for piece in shares])

    source = slot_source[0]
    filled = source >= 0
    sender = jnp.where(filled, source // tokens, -1)
    place = jnp.where(filled, source % tokens, 0)
    patch = jnp.arange(merge * slots, dtype=jnp.int32)
    sender_patch = jnp.repeat(sender, merge)
    by_sender = (sender_patch[None, :] == patch[:, None] // merge) & (
        patch[None, :] % merge == patch[:, None] % merge
    )
    outgoing = select(saved_early[0], by_sender)
    device = jnp.arange(devices, dtype=jnp.int32)
    wanted = jnp.sum(
        jnp.where(sender[None, :] == device[:, None], place[None, :] + 1, 0), axis=1
    )
    tag = jnp.broadcast_to(wanted[:, None, None], (devices, merge, 128)).astype(BF16)
    message = jnp.concatenate([outgoing.reshape(devices, merge, width), tag], axis=2)
    arrived = lax.all_to_all(message, CTX, 0, 0, tiled=True)
    asked = arrived[:, 0, width].astype(jnp.int32) - 1
    asked_patch = jnp.repeat(asked, merge)
    token_patch = jnp.arange(merge * tokens, dtype=jnp.int32)
    by_token = (asked_patch[None, :] == token_patch[:, None] // merge) & (
        patch[None, :] % merge == token_patch[:, None] % merge
    )
    saved_rows = select(arrived[:, :, :width].reshape(devices * merge, width), by_token)

    rows = jnp.concatenate([early, middle, late], axis=1)
    packed = select(rows, by_token.T).reshape(devices, merge, 3 * width)
    landed = lax.all_to_all(packed, CTX, 0, 0, tiled=True).reshape(devices * merge, 3 * width)

    saved = [saved_rows] + [over_x(saved_rows, step) for step in (1, 2, 3)]
    kept, given = gradient(saved, keep, give)
    partial = (kept + over_core(given).astype(F32)).astype(BF16)
    terms = lax.all_to_all(
        partial.reshape(devices, width // devices * share), CTX, 0, 0, tiled=True
    )
    weights = jnp.sum(terms.astype(F32), axis=0).reshape(width // devices, share)

    context_early, context_middle, context_late, stream = contexts(
        jnp.stack([x, core]).astype(jnp.int32),
        by_sender.T.astype(BF16),
        landed,
        pieces,
        shard,
        cut,
    )
    return context_early[None], context_middle[None], context_late[None], stream[None], weights


def solution(mesh):
    fine = Mesh(mesh.devices.reshape(4, 2, 8, 4), ("x", "core", "z", "y"))
    rows = P(DP, CTX, None)
    return jax.shard_map(
        local,
        mesh=fine,
        in_specs=(rows, rows, rows, P(DP, CTX), rows, P(DP, None), P(DP, None), P(DP, None)),
        out_specs=(rows, rows, rows, rows, P(CTX, DP)),
        check_vma=False,
    )
```

```python
import jax
import jax.numpy as jnp
from jax import lax
from jax.experimental import pallas as pl
from jax.experimental.pallas import tpu as pltpu
from jax.sharding import Mesh, PartitionSpec as P

DP = ("x", "core")
CTX = ("z", "y")
BF16 = jnp.bfloat16
F32 = jnp.float32
VMEM = pl.BlockSpec(memory_space=pltpu.VMEM)
SMEM = pl.BlockSpec(memory_space=pltpu.SMEM)
ANY = pl.BlockSpec(memory_space=pl.ANY)
PARAMS = pltpu.CompilerParams(vmem_limit_bytes=32 << 20)

WIDTH = 1152
MERGE = 4
TOKENS = 20
SLOTS = 32
SHARD = 144
OWN = 36
SAVED_HALF = 640
ROWS_HALF = 1792
TERM_ROWS = 48
REST = 5


def over_x(array, step):
    return lax.ppermute(array, "x", [(i, (i + step) % 4) for i in range(4)])


def over_core(array):
    return lax.ppermute(array, "core", [(0, 1), (1, 0)])


def iota(shape, dim):
    return lax.broadcasted_iota(jnp.int32, shape, dim)


def onehot(condition):
    return jnp.where(condition, 1.0, 0.0).astype(BF16)


def matmul(a, b):
    return jnp.dot(a, b, preferred_element_type=F32)


def matmul_tn(a, b):
    return lax.dot_general(a, b, (((0,), (0,)), ((), ())), preferred_element_type=F32)


def quotient(value, by):
    return jnp.floor((value + 0.5) * (1.0 / by))


def message_kernel(slot_ref, saved_ref, message_ref, table_ref):
    source = slot_ref[...].astype(F32)
    sender = quotient(source, TOKENS)
    place = source - TOKENS * sender
    both = jnp.where(iota((8, SLOTS), 0) == 0, sender, place).astype(BF16)
    repeat = onehot(iota((SLOTS, SLOTS * MERGE), 1) // MERGE == iota((SLOTS, SLOTS * MERGE), 0))
    wide = matmul(both, repeat)
    sender, place = wide[0:1], wide[1:2]
    shape = (8 * SLOTS, MERGE * SLOTS)
    row, column = iota(shape, 0), iota(shape, 1)
    match = (sender == (row // 8).astype(F32)) & (row % MERGE == column % MERGE)
    first = match & (row % 8 < MERGE)
    second = match & (row % 8 >= MERGE)
    tag = jnp.sum(jnp.where(second, place + 1.0, 0.0), axis=1, keepdims=True)
    first, second = onehot(first), onehot(second)
    table_ref[:, : MERGE * SLOTS] = first
    table_ref[:, MERGE * SLOTS :] = second
    rest = WIDTH - SAVED_HALF
    left = matmul(first, saved_ref[:, :SAVED_HALF])
    right = matmul(second, saved_ref[:, SAVED_HALF:])
    message = jnp.concatenate([left[:, :rest] + right, left[:, rest:] + tag], axis=1)
    message_ref[...] = message.reshape(SLOTS, 8, SAVED_HALF).astype(BF16)


def make_message(slot, saved):
    return pl.pallas_call(
        message_kernel,
        out_shape=(
            jax.ShapeDtypeStruct((SLOTS, 8, SAVED_HALF), BF16),
            jax.ShapeDtypeStruct((8 * SLOTS, 2 * MERGE * SLOTS), BF16),
        ),
        in_specs=[VMEM] * 2,
        out_specs=(VMEM,) * 2,
        compiler_params=PARAMS,
    )(slot, saved)


def rows_kernel(at_ref, early_ref, middle_ref, late_ref, rows_ref, keep_ref, give_ref, sums):
    x, core = at_ref[0], at_ref[1]
    used = MERGE * TOKENS
    for j in range(MERGE):
        at = slice(j * WIDTH, (j + 1) * WIDTH)
        to = slice(j * TOKENS, (j + 1) * TOKENS)
        late = late_ref[:, at].astype(F32)
        middle = late + middle_ref[:, at].astype(F32)
        sums[to, 2 * WIDTH : 3 * WIDTH] = late
        sums[to, WIDTH : 2 * WIDTH] = middle
        sums[to, :WIDTH] = middle + early_ref[:, at].astype(F32)
    rows_ref[...] = jnp.zeros_like(rows_ref)
    rows_ref[:used, : 3 * WIDTH] = sums[...].astype(BF16)
    early = sums[:, :WIDTH]
    for d in range(8):
        main = early[:, d * SHARD : d * SHARD + 128]
        rest = early[:, d * SHARD + 128 : (d + 1) * SHARD]
        piece = jnp.concatenate([main] + [rest] * 8, axis=1).astype(BF16)
        step = lax.rem(d // 2 + 4 - x, 4)

        @pl.when(core == d % 2)
        def _():
            keep_ref[step] = piece

        @pl.when(core != d % 2)
        def _():
            give_ref[step] = piece


def make_rows(at, early, middle, late):
    piece = jax.ShapeDtypeStruct((4, MERGE * TOKENS, 256), BF16)
    return pl.pallas_call(
        rows_kernel,
        out_shape=(jax.ShapeDtypeStruct((128, 2 * ROWS_HALF), BF16), piece, piece),
        in_specs=[SMEM] + [VMEM] * 3,
        out_specs=(VMEM,) * 3,
        scratch_shapes=[pltpu.VMEM((MERGE * TOKENS, 3 * WIDTH), F32)],
        compiler_params=PARAMS,
    )(at, early, middle, late)


def pack_kernel(arrived_ref, rows_ref, saved_ref, packed_ref):
    count = 8 * SLOTS
    arrived = arrived_ref[...].astype(F32).reshape(count, SAVED_HALF).astype(BF16)
    rest = WIDTH - SAVED_HALF
    row, column = iota((count, count), 0), iota((count, count), 1)
    spread = onehot((row // 8 == column // 8) & (column % 8 == MERGE))
    asked = matmul(spread, arrived[:, rest:])
    row, column = iota((count, 128), 0), iota((count, 128), 1)
    j = sum((column >= k * TOKENS).astype(jnp.int32) for k in range(1, MERGE + 1))
    token = (column - TOKENS * j + 1).astype(F32)
    match = (asked == token) & (row % MERGE == j)
    first = onehot(match & (row % 8 < MERGE))
    second = onehot(match & (row % 8 >= MERGE))
    packed = matmul(first, rows_ref[:, :ROWS_HALF]) + matmul(second, rows_ref[:, ROWS_HALF:])
    packed_ref[...] = packed.reshape(SLOTS, 8, ROWS_HALF).astype(BF16)
    used = MERGE * TOKENS
    saved_ref[:, :SAVED_HALF] = matmul_tn(first, arrived)[:used].astype(BF16)
    saved_ref[:, SAVED_HALF:] = matmul_tn(second, arrived[:, :rest])[:used].astype(BF16)


def pack(arrived, rows):
    return pl.pallas_call(
        pack_kernel,
        out_shape=(
            jax.ShapeDtypeStruct((MERGE * TOKENS, WIDTH), BF16),
            jax.ShapeDtypeStruct((SLOTS, 8, ROWS_HALF), BF16),
        ),
        in_specs=[VMEM] * 2,
        out_specs=(VMEM,) * 2,
        compiler_params=PARAMS,
    )(arrived, rows)


def gradient_kernel(*refs):
    own, other, columns = refs[:4], refs[4:8], refs[8:12]
    terms_ref, product = refs[12:]
    saved = jnp.concatenate([ref[...] for k in range(4) for ref in (own[k], other[k])], axis=0)
    product[...] = matmul_tn(saved, jnp.concatenate([ref[...] for ref in columns], axis=0))
    line = iota((WIDTH, 128), 0).astype(F32)
    inside = line - OWN * quotient(line, OWN)
    group = (iota((WIDTH, 128), 1) // 16).astype(F32)
    rest = jnp.where(inside - 8 * quotient(inside, 8) == group, product[:, 128:], 0.0)
    line = iota((1, WIDTH), 1).astype(F32)
    block = quotient(line, OWN)
    to = REST * block + quotient(line - OWN * block, 8)
    fold = onehot(iota((REST * SLOTS, WIDTH), 0).astype(F32) == to)
    folded = matmul(fold, rest.astype(BF16))
    fill = jnp.zeros((TERM_ROWS - OWN - REST, 128), F32)
    for c in range(SLOTS):
        main = product[c * OWN : (c + 1) * OWN, :128]
        message = jnp.concatenate([main, folded[c * REST : (c + 1) * REST], fill], axis=0)
        terms_ref[c] = message.astype(BF16)


def gradient(own, other, columns):
    return pl.pallas_call(
        gradient_kernel,
        out_shape=jax.ShapeDtypeStruct((SLOTS, TERM_ROWS, 128), BF16),
        in_specs=[VMEM] * 12,
        out_specs=VMEM,
        scratch_shapes=[pltpu.VMEM((WIDTH, 256), F32)],
        compiler_params=PARAMS,
    )(*own, *other, *columns)


def total_kernel(terms_ref, out_ref):
    total = terms_ref[0].astype(F32)
    for c in range(1, SLOTS):
        total = total + terms_ref[c].astype(F32)
    rest = jnp.concatenate(
        [jnp.broadcast_to(total[OWN + a : OWN + a + 1], (8, 128)) for a in range(REST)], axis=0
    )[:OWN]
    line, column = iota((OWN, 128), 0), iota((OWN, 128), 1)
    rest = jnp.where(line % 8 == column // 16, rest, 0.0)
    for shift in (64, 32, 16):
        rest = rest + pltpu.roll(rest, shift, 1)
    out_ref[:, :128] = total[:OWN]
    out_ref[:, 128:] = rest[:, : SHARD - 128]


def add_up(terms):
    return pl.pallas_call(
        total_kernel,
        out_shape=jax.ShapeDtypeStruct((OWN, SHARD), F32),
        in_specs=[VMEM],
        out_specs=VMEM,
        compiler_params=PARAMS,
    )(terms)


def context_kernel(cut, at_ref, table_ref, landed_ref, *refs):
    pieces = refs[:10]
    early_out, middle_out, late_out, stream_out, weight, sem = refs[10:]
    x, core = at_ref[0], at_ref[1]
    copies = ([], [], [])

    def put(ref, first, rows, m, inside, of_x, of_core):
        base = pl.multiple_of((2 * of_x + of_core) * SHARD + inside, 16)
        copies[m].append(
            pltpu.make_async_copy(
                ref.at[pl.ds(first, rows)], weight.at[m, pl.ds(base, rows)], sem.at[m]
            )
        )

    for index, of_core in ((0, core), (5, 1 - core)):
        for k, step in enumerate((0, 3, 1)):
            for m in range(3):
                put(pieces[index + k], m * SHARD, SHARD, m, 0, lax.rem(x + step, 4), of_core)
        of_x = lax.rem(x + 2, 4)
        for ref, start, stop in ((pieces[index + 3], 0, cut), (pieces[index + 4], cut, 3 * SHARD)):
            for m in range(3):
                low, high = max(start, m * SHARD), min(stop, (m + 1) * SHARD)
                if low < high:
                    put(ref, low - start, high - low, m, low - m * SHARD, of_x, of_core)
    for m in range(3):
        for copy in copies[m]:
            copy.start()
    landed = landed_ref[...].astype(F32).reshape(8 * SLOTS, ROWS_HALF).astype(BF16)
    placed = matmul_tn(table_ref[...], landed).astype(BF16)
    half = MERGE * SLOTS
    placed = jnp.concatenate([placed[:half], placed[half:, : 3 * WIDTH - ROWS_HALF]], axis=1)
    stream_out[...] = placed[:, :WIDTH]
    for m, out in enumerate((early_out, middle_out, late_out)):
        for copy in copies[m]:
            copy.wait()
        out[...] = lax.dot_general(
            placed[:, m * WIDTH : (m + 1) * WIDTH],
            weight[m],
            (((1,), (1,)), ((), ())),
            preferred_element_type=F32,
        ).astype(BF16)


def contexts(at, table, landed, pieces, cut):
    rows = MERGE * SLOTS
    out = jax.ShapeDtypeStruct((rows, WIDTH), BF16)
    return pl.pallas_call(
        lambda *refs: context_kernel(cut, *refs),
        out_shape=(out,) * 4,
        in_specs=[SMEM, VMEM, VMEM] + [ANY] * 10,
        out_specs=(VMEM,) * 4,
        scratch_shapes=[
            pltpu.VMEM((3, WIDTH, WIDTH), BF16),
            pltpu.SemaphoreType.DMA((3,)),
        ],
        compiler_params=PARAMS,
        cost_estimate=pl.CostEstimate(
            flops=6 * rows * WIDTH * WIDTH, bytes_accessed=6 * WIDTH * WIDTH, transcendentals=0
        ),
    )(at, table, landed, *pieces)


def local(
    injected_early,
    injected_middle,
    injected_late,
    slot_source,
    saved_early,
    projection_early,
    projection_middle,
    projection_late,
):
    at = jnp.stack([lax.axis_index("x"), lax.axis_index("core")]).astype(jnp.int32)

    message, table = make_message(slot_source, saved_early[0])
    arrived = lax.all_to_all(message, CTX, 0, 0, tiled=True)

    stacked = jnp.concatenate([projection_early, projection_middle, projection_late])
    cut = 224
    from_left, from_right = over_x(stacked, 1), over_x(stacked, 3)
    rows, keep, give = make_rows(at, injected_early[0], injected_middle[0], injected_late[0])
    arrived, rows, from_left, from_right = lax.optimization_barrier(
        (arrived, rows, from_left, from_right)
    )
    far_left, far_right = over_x(from_left[:cut], 1), over_x(from_right[cut:], 3)
    pieces = (stacked, from_left, from_right, far_left, far_right)
    pieces = pieces + tuple(over_core(piece) for piece in pieces)

    given = over_core(give)
    mixed = [jnp.concatenate([keep[step], given[step]]) for step in range(4)]
    columns = [mixed[0]] + [over_x(mixed[step], step) for step in (1, 2, 3)]

    saved_rows, packed = pack(arrived, rows)
    landed = lax.all_to_all(packed, CTX, 0, 0, tiled=True)

    own = [saved_rows] + [over_x(saved_rows, step) for step in (1, 2, 3)]
    other = [over_core(piece) for piece in own]
    own, other, columns, landed = lax.optimization_barrier((own, other, columns, landed))
    terms = lax.all_to_all(gradient(own, other, columns), CTX, 0, 0, tiled=True)
    weights = add_up(terms)

    context_early, context_middle, context_late, stream = contexts(at, table, landed, pieces, cut)
    return context_early[None], context_middle[None], context_late[None], stream[None], weights


def solution(mesh):
    fine = Mesh(mesh.devices.reshape(4, 2, 8, 4), ("x", "core", "z", "y"))
    rows = P(DP, CTX, None)
    return jax.shard_map(
        local,
        mesh=fine,
        in_specs=(rows, rows, rows, P(DP, CTX), rows, P(DP, None), P(DP, None), P(DP, None)),
        out_specs=(rows, rows, rows, rows, P(CTX, DP)),
        check_vma=False,
    )
```

```python
import jax
import jax.numpy as jnp
from jax import lax
from jax.experimental import pallas as pl
from jax.experimental.pallas import tpu as pltpu
from jax.sharding import Mesh, PartitionSpec as P

DP = ("x", "core")
CTX = ("z", "y")
BF16 = jnp.bfloat16
F32 = jnp.float32
VMEM = pl.BlockSpec(memory_space=pltpu.VMEM)
SMEM = pl.BlockSpec(memory_space=pltpu.SMEM)
ANY = pl.BlockSpec(memory_space=pl.ANY)
PARAMS = pltpu.CompilerParams(vmem_limit_bytes=32 << 20)

WIDTH = 1152
MERGE = 4
TOKENS = 20
SLOTS = 32
SHARD = 144
OWN = 36
SAVED_HALF = 640
ROWS_HALF = 1792
TERM_ROWS = 48
REST = 5


def over_x(array, step):
    return lax.ppermute(array, "x", [(i, (i + step) % 4) for i in range(4)])


def over_y(array, step):
    return lax.ppermute(array, "y", [(i, (i + step) % 4) for i in range(4)])


def over_core(array):
    return lax.ppermute(array, "core", [(0, 1), (1, 0)])


def iota(shape, dim):
    return lax.broadcasted_iota(jnp.int32, shape, dim)


def onehot(condition):
    return jnp.where(condition, 1.0, 0.0).astype(BF16)


def matmul(a, b):
    return jnp.dot(a, b, preferred_element_type=F32)


def matmul_tn(a, b):
    return lax.dot_general(a, b, (((0,), (0,)), ((), ())), preferred_element_type=F32)


def quotient(value, by):
    return jnp.floor((value + 0.5) * (1.0 / by))


def message_kernel(
    slot_ref, saved_hbm, early, middle, late, message_ref, table_ref, stacked, saved_ref, sem
):
    fetch = pltpu.make_async_copy(saved_hbm, saved_ref, sem.at[3])
    fetch.start()
    stack = [
        pltpu.make_async_copy(ref, stacked.at[pl.ds(m * SHARD, SHARD)], sem.at[m])
        for m, ref in enumerate((early, middle, late))
    ]
    for copy in stack:
        copy.start()
    source = slot_ref[...].astype(F32)
    sender = quotient(source, TOKENS)
    place = source - TOKENS * sender
    both = jnp.where(iota((8, SLOTS), 0) == 0, sender, place).astype(BF16)
    repeat = onehot(iota((SLOTS, SLOTS * MERGE), 1) // MERGE == iota((SLOTS, SLOTS * MERGE), 0))
    wide = matmul(both, repeat)
    sender, place = wide[0:1], wide[1:2]
    shape = (8 * SLOTS, MERGE * SLOTS)
    row, column = iota(shape, 0), iota(shape, 1)
    match = (sender == (row // 8).astype(F32)) & (row % MERGE == column % MERGE)
    first = match & (row % 8 < MERGE)
    second = match & (row % 8 >= MERGE)
    tag = jnp.sum(jnp.where(second, place + 1.0, 0.0), axis=1, keepdims=True)
    first, second = onehot(first), onehot(second)
    table_ref[:, : MERGE * SLOTS] = first
    table_ref[:, MERGE * SLOTS :] = second
    rest = WIDTH - SAVED_HALF
    fetch.wait()
    left = matmul(first, saved_ref[:, :SAVED_HALF])
    right = matmul(second, saved_ref[:, SAVED_HALF:])
    message = jnp.concatenate([left[:, :rest] + right, left[:, rest:] + tag], axis=1)
    message_ref[...] = message.reshape(SLOTS, 8, SAVED_HALF).astype(BF16)
    for copy in stack:
        copy.wait()


def make_message(slot, saved, projections):
    return pl.pallas_call(
        message_kernel,
        out_shape=(
            jax.ShapeDtypeStruct((SLOTS, 8, SAVED_HALF), BF16),
            jax.ShapeDtypeStruct((8 * SLOTS, 2 * MERGE * SLOTS), BF16),
            jax.ShapeDtypeStruct((3 * SHARD, WIDTH), BF16),
        ),
        in_specs=[VMEM] + [ANY] * 4,
        out_specs=(VMEM, VMEM, ANY),
        scratch_shapes=[
            pltpu.VMEM((MERGE * SLOTS, WIDTH), BF16),
            pltpu.SemaphoreType.DMA((4,)),
        ],
        compiler_params=PARAMS,
    )(slot, saved, *projections)


def rows_kernel(at_ref, early_ref, middle_ref, late_ref, rows_ref, keep_ref, give_ref, sums):
    x, core = at_ref[0], at_ref[1]
    used = MERGE * TOKENS
    for j in range(MERGE):
        at = slice(j * WIDTH, (j + 1) * WIDTH)
        to = slice(j * TOKENS, (j + 1) * TOKENS)
        late = late_ref[:, at].astype(F32)
        middle = late + middle_ref[:, at].astype(F32)
        sums[to, 2 * WIDTH : 3 * WIDTH] = late
        sums[to, WIDTH : 2 * WIDTH] = middle
        sums[to, :WIDTH] = middle + early_ref[:, at].astype(F32)
    rows_ref[...] = jnp.zeros_like(rows_ref)
    rows_ref[:used, : 3 * WIDTH] = sums[...].astype(BF16)
    early = sums[:, :WIDTH]
    for d in range(8):
        main = early[:, d * SHARD : d * SHARD + 128]
        rest = early[:, d * SHARD + 128 : (d + 1) * SHARD]
        piece = jnp.concatenate([main] + [rest] * 8, axis=1).astype(BF16)
        step = lax.rem(d // 2 + 4 - x, 4)

        @pl.when(core == d % 2)
        def _():
            keep_ref[step] = piece

        @pl.when(core != d % 2)
        def _():
            give_ref[step] = piece


def make_rows(at, early, middle, late):
    piece = jax.ShapeDtypeStruct((4, MERGE * TOKENS, 256), BF16)
    return pl.pallas_call(
        rows_kernel,
        out_shape=(jax.ShapeDtypeStruct((128, 2 * ROWS_HALF), BF16), piece, piece),
        in_specs=[SMEM] + [VMEM] * 3,
        out_specs=(VMEM,) * 3,
        scratch_shapes=[pltpu.VMEM((MERGE * TOKENS, 3 * WIDTH), F32)],
        compiler_params=PARAMS,
    )(at, early, middle, late)


def unpack_kernel(arrived_ref, saved_ref, table_ref):
    count = 8 * SLOTS
    arrived = arrived_ref[...].astype(F32).reshape(count, SAVED_HALF).astype(BF16)
    rest = WIDTH - SAVED_HALF
    row, column = iota((count, count), 0), iota((count, count), 1)
    spread = onehot((row // 8 == column // 8) & (column % 8 == MERGE))
    asked = matmul(spread, arrived[:, rest:])
    row, column = iota((count, 128), 0), iota((count, 128), 1)
    j = sum((column >= k * TOKENS).astype(jnp.int32) for k in range(1, MERGE + 1))
    token = (column - TOKENS * j + 1).astype(F32)
    match = (asked == token) & (row % MERGE == j)
    first = onehot(match & (row % 8 < MERGE))
    second = onehot(match & (row % 8 >= MERGE))
    table_ref[:, :128] = first
    table_ref[:, 128:] = second
    used = MERGE * TOKENS
    saved_ref[:, :SAVED_HALF] = matmul_tn(first, arrived)[:used].astype(BF16)
    saved_ref[:, SAVED_HALF:] = matmul_tn(second, arrived[:, :rest])[:used].astype(BF16)


def unpack(arrived):
    return pl.pallas_call(
        unpack_kernel,
        out_shape=(
            jax.ShapeDtypeStruct((MERGE * TOKENS, WIDTH), BF16),
            jax.ShapeDtypeStruct((8 * SLOTS, 256), BF16),
        ),
        in_specs=[VMEM],
        out_specs=(VMEM,) * 2,
        compiler_params=PARAMS,
    )(arrived)


def pack_kernel(table_ref, rows_ref, packed_ref):
    packed = matmul(table_ref[:, :128], rows_ref[:, :ROWS_HALF])
    packed = packed + matmul(table_ref[:, 128:], rows_ref[:, ROWS_HALF:])
    packed_ref[...] = packed.reshape(SLOTS, 8, ROWS_HALF).astype(BF16)


def pack(table, rows):
    return pl.pallas_call(
        pack_kernel,
        out_shape=jax.ShapeDtypeStruct((SLOTS, 8, ROWS_HALF), BF16),
        in_specs=[VMEM] * 2,
        out_specs=VMEM,
        compiler_params=PARAMS,
    )(table, rows)


def gradient_kernel(y_ref, *refs):
    pieces, (own_ref, *out_refs), (saved, columns, product, folded, terms, sem) = (
        refs[:12],
        refs[12:16],
        refs[16:],
    )
    rows = MERGE * TOKENS
    copies = []
    for k, ref in enumerate(pieces):
        if k < 8:
            to = saved.at[pl.ds(k * rows, rows)]
        else:
            to = columns.at[pl.ds((k - 8) * 2 * rows, 2 * rows)]
        copies.append(pltpu.make_async_copy(ref, to, sem.at[k]))
    for copy in copies:
        copy.start()
    line = iota((WIDTH, 128), 0).astype(F32)
    inside = line - OWN * quotient(line, OWN)
    group = (iota((WIDTH, 128), 1) // 16).astype(F32)
    mine = inside - 8 * quotient(inside, 8) == group
    line = iota((1, WIDTH), 1).astype(F32)
    block = quotient(line, OWN)
    to = REST * block + quotient(line - OWN * block, 8)
    fold = onehot(iota((REST * SLOTS, WIDTH), 0).astype(F32) == to)
    for copy in copies:
        copy.wait()
    product[...] = matmul_tn(saved[...], columns[...])
    folded[...] = matmul(fold, jnp.where(mine, product[:, 128:], 0.0).astype(BF16))
    fill = jnp.zeros((TERM_ROWS - OWN - REST, 128), F32)
    for c in range(SLOTS):
        step = lax.rem(c % 4 + 4 - y_ref[0], 4)
        parts = [product[c * OWN : (c + 1) * OWN, :128], folded[c * REST : (c + 1) * REST], fill]
        terms[step, c // 4] = jnp.concatenate(parts, axis=0)
    for step, out in enumerate((own_ref, *out_refs)):
        out[...] = terms[step].astype(out.dtype)


def gradient(y, own, other, columns):
    shape = (8, TERM_ROWS, 128)
    return pl.pallas_call(
        gradient_kernel,
        out_shape=[jax.ShapeDtypeStruct(shape, F32)] + [jax.ShapeDtypeStruct(shape, BF16)] * 3,
        in_specs=[SMEM] + [ANY] * 12,
        out_specs=[VMEM] * 4,
        scratch_shapes=[
            pltpu.VMEM((8 * MERGE * TOKENS, WIDTH), BF16),
            pltpu.VMEM((8 * MERGE * TOKENS, 256), BF16),
            pltpu.VMEM((WIDTH, 256), F32),
            pltpu.VMEM((REST * SLOTS, 128), F32),
            pltpu.VMEM((4, 8, TERM_ROWS, 128), F32),
            pltpu.SemaphoreType.DMA((12,)),
        ],
        compiler_params=PARAMS,
    )(y, *(piece for pair in zip(own, other) for piece in pair), *columns)


def sum_kernel(own_ref, first, second, third, out_ref):
    total = own_ref[...]
    for ref in (first, second, third):
        total = total + ref[...].astype(F32)
    out_ref[...] = total.astype(BF16)


def sum_y(own, parts):
    return pl.pallas_call(
        sum_kernel,
        out_shape=jax.ShapeDtypeStruct(own.shape, BF16),
        in_specs=[VMEM] * 4,
        out_specs=VMEM,
        compiler_params=PARAMS,
    )(own, *parts)


def total_kernel(terms_ref, out_ref):
    total = terms_ref[0].astype(F32)
    for c in range(1, 8):
        total = total + terms_ref[c].astype(F32)
    rest = jnp.concatenate(
        [jnp.broadcast_to(total[OWN + a : OWN + a + 1], (8, 128)) for a in range(REST)], axis=0
    )[:OWN]
    line, column = iota((OWN, 128), 0), iota((OWN, 128), 1)
    rest = jnp.where(line % 8 == column // 16, rest, 0.0)
    for shift in (64, 32, 16):
        rest = rest + pltpu.roll(rest, shift, 1)
    out_ref[:, :128] = total[:OWN]
    out_ref[:, 128:] = rest[:, : SHARD - 128]


def add_up(terms):
    return pl.pallas_call(
        total_kernel,
        out_shape=jax.ShapeDtypeStruct((OWN, SHARD), F32),
        in_specs=[VMEM],
        out_specs=VMEM,
        compiler_params=PARAMS,
    )(terms)


def context_kernel(cut, at_ref, table_ref, landed_ref, *refs):
    pieces = refs[:10]
    early_out, middle_out, late_out, stream_out, weight, sem = refs[10:]
    x, core = at_ref[0], at_ref[1]
    copies = ([], [], [])

    def put(ref, first, rows, m, inside, of_x, of_core):
        base = pl.multiple_of((2 * of_x + of_core) * SHARD + inside, 16)
        copies[m].append(
            pltpu.make_async_copy(
                ref.at[pl.ds(first, rows)], weight.at[m, pl.ds(base, rows)], sem.at[m]
            )
        )

    for index, of_core in ((0, core), (5, 1 - core)):
        for k, step in enumerate((0, 3, 1)):
            for m in range(3):
                put(pieces[index + k], m * SHARD, SHARD, m, 0, lax.rem(x + step, 4), of_core)
        of_x = lax.rem(x + 2, 4)
        for ref, start, stop in ((pieces[index + 3], 0, cut), (pieces[index + 4], cut, 3 * SHARD)):
            for m in range(3):
                low, high = max(start, m * SHARD), min(stop, (m + 1) * SHARD)
                if low < high:
                    put(ref, low - start, high - low, m, low - m * SHARD, of_x, of_core)
    for m in range(3):
        for copy in copies[m]:
            copy.start()
    landed = landed_ref[...].astype(F32).reshape(8 * SLOTS, ROWS_HALF).astype(BF16)
    placed = matmul_tn(table_ref[...], landed).astype(BF16)
    half = MERGE * SLOTS
    placed = jnp.concatenate([placed[:half], placed[half:, : 3 * WIDTH - ROWS_HALF]], axis=1)
    stream_out[...] = placed[:, :WIDTH]
    for m, out in enumerate((early_out, middle_out, late_out)):
        for copy in copies[m]:
            copy.wait()
        out[...] = lax.dot_general(
            placed[:, m * WIDTH : (m + 1) * WIDTH],
            weight[m],
            (((1,), (1,)), ((), ())),
            preferred_element_type=F32,
        ).astype(BF16)


def contexts(at, table, landed, pieces, cut):
    rows = MERGE * SLOTS
    out = jax.ShapeDtypeStruct((rows, WIDTH), BF16)
    return pl.pallas_call(
        lambda *refs: context_kernel(cut, *refs),
        out_shape=(out,) * 4,
        in_specs=[SMEM, VMEM, VMEM] + [ANY] * 10,
        out_specs=(VMEM,) * 4,
        scratch_shapes=[
            pltpu.VMEM((3, WIDTH, WIDTH), BF16),
            pltpu.SemaphoreType.DMA((3,)),
        ],
        compiler_params=PARAMS,
        cost_estimate=pl.CostEstimate(
            flops=6 * rows * WIDTH * WIDTH, bytes_accessed=6 * WIDTH * WIDTH, transcendentals=0
        ),
    )(at, table, landed, *pieces)


def local(
    injected_early,
    injected_middle,
    injected_late,
    slot_source,
    saved_early,
    projection_early,
    projection_middle,
    projection_late,
):
    at = jnp.stack([lax.axis_index("x"), lax.axis_index("core")]).astype(jnp.int32)
    y = lax.axis_index("y").astype(jnp.int32).reshape(1)

    projections = (projection_early, projection_middle, projection_late)
    message, table, stacked = make_message(slot_source, saved_early[0], projections)
    arrived = lax.all_to_all(message, CTX, 0, 0, tiled=True)

    cut = 224
    from_left, from_right = over_x(stacked, 1), over_x(stacked, 3)

    rows, keep, give = make_rows(at, injected_early[0], injected_middle[0], injected_late[0])
    given = over_core(give)
    mixed = [jnp.concatenate([keep[step], given[step]]) for step in range(4)]
    columns = [mixed[0]] + [over_x(mixed[step], step) for step in (1, 2, 3)]
    arrived, from_left, from_right, columns = lax.optimization_barrier(
        (arrived, from_left, from_right, columns)
    )

    saved_rows, by_token = unpack(arrived)
    own = [saved_rows] + [over_x(saved_rows, step) for step in (1, 2, 3)]
    landed = lax.all_to_all(pack(by_token, rows), CTX, 0, 0, tiled=True)

    own, from_left, from_right = lax.optimization_barrier((own, from_left, from_right))
    far_left, far_right = over_x(from_left[:cut], 1), over_x(from_right[cut:], 3)
    pieces = (stacked, from_left, from_right, far_left, far_right)
    pieces = pieces + tuple(over_core(piece) for piece in pieces)

    other = [over_core(piece) for piece in own]
    mine, *parts = gradient(y, own, other, columns)
    parts = [over_y(part, step) for step, part in zip((1, 2, 3), parts)]
    terms = sum_y(mine, parts)
    terms, landed = lax.optimization_barrier((terms, landed))
    weights = add_up(lax.all_to_all(terms, "z", 0, 0, tiled=True))

    context_early, context_middle, context_late, stream = contexts(at, table, landed, pieces, cut)
    return context_early[None], context_middle[None], context_late[None], stream[None], weights


def solution(mesh):
    fine = Mesh(mesh.devices.reshape(4, 2, 8, 4), ("x", "core", "z", "y"))
    rows = P(DP, CTX, None)
    return jax.shard_map(
        local,
        mesh=fine,
        in_specs=(rows, rows, rows, P(DP, CTX), rows, P(DP, None), P(DP, None), P(DP, None)),
        out_specs=(rows, rows, rows, rows, P(CTX, DP)),
        check_vma=False,
    )
```

```python
import jax
import jax.numpy as jnp
from jax import lax
from jax.experimental import pallas as pl
from jax.experimental.pallas import tpu as pltpu
from jax.sharding import Mesh, PartitionSpec as P

DP = ("x", "core")
CTX = ("z", "y")
BF16 = jnp.bfloat16
F32 = jnp.float32
VMEM = pl.BlockSpec(memory_space=pltpu.VMEM)
SMEM = pl.BlockSpec(memory_space=pltpu.SMEM)
HBM = pl.BlockSpec(memory_space=pltpu.HBM)
PARAMS = pltpu.CompilerParams(vmem_limit_bytes=32 << 20)

WIDTH = 1152
MERGE = 4
TOKENS = 20
SLOTS = 32
SHARD = 144
OWN = 36
QUARTER = 288
SAVED_WIDE = 384
SAVED_ROWS = 16
FIRST = 32
ROWS_HALF = 1792
TERM_ROWS = 48
REST = 5


def over_x(array, step):
    return lax.ppermute(array, "x", [(i, (i + step) % 4) for i in range(4)])


def over_y(array, step):
    return lax.ppermute(array, "y", [(i, (i + step) % 4) for i in range(4)])


def over_core(array):
    return lax.ppermute(array, "core", [(0, 1), (1, 0)])


def iota(shape, dim):
    return lax.broadcasted_iota(jnp.int32, shape, dim)


def onehot(condition):
    return jnp.where(condition, 1.0, 0.0).astype(BF16)


def matmul(a, b):
    return jnp.dot(a, b, preferred_element_type=F32)


def matmul_tn(a, b):
    return lax.dot_general(a, b, (((0,), (0,)), ((), ())), preferred_element_type=F32)


def quotient(value, by):
    return jnp.floor((value + 0.5) * (1.0 / by))


def message_kernel(
    slot_ref, saved_hbm, early, middle, late, message_ref, table_ref, stacked, saved_ref, sem
):
    fetch = pltpu.make_async_copy(saved_hbm, saved_ref, sem.at[3])
    fetch.start()
    stack = [
        pltpu.make_async_copy(ref, stacked.at[pl.ds(m * SHARD, SHARD)], sem.at[m])
        for m, ref in enumerate((early, middle, late))
    ]
    for copy in stack:
        copy.start()
    source = slot_ref[...].astype(F32)
    sender = quotient(source, TOKENS)
    place = source - TOKENS * sender
    both = jnp.where(iota((8, SLOTS), 0) == 0, sender, place).astype(BF16)
    repeat = onehot(iota((SLOTS, SLOTS * MERGE), 1) // MERGE == iota((SLOTS, SLOTS * MERGE), 0))
    wide = matmul(both, repeat)
    sender, place = wide[0:1], wide[1:2]
    count = MERGE * SLOTS
    row, column = iota((count, count), 0), iota((count, count), 1)
    match = (sender == (row // MERGE).astype(F32)) & (row % MERGE == column % MERGE)
    tag = jnp.sum(jnp.where(match, place + 1.0, 0.0), axis=1, keepdims=True)
    tag = jnp.broadcast_to(tag, (count, SAVED_WIDE - QUARTER))
    match = onehot(match)
    fetch.wait()
    sorted_rows = matmul(match, saved_ref[...])
    for y in range(4):
        blocks = [sorted_rows[:, OWN * c : OWN * (c + 1)] for c in range(y, SLOTS, 4)]
        message = jnp.concatenate(blocks + [tag], axis=1).astype(BF16)
        for z in range(8):
            message_ref[4 * z + y] = message[SAVED_ROWS * z : SAVED_ROWS * (z + 1)]
    row, column = iota((2 * count, count), 0), iota((2 * count, count), 1)
    match = (sender == (row // 8).astype(F32)) & (row % MERGE == column % MERGE)
    table_ref[:, :count] = onehot(match & (row % 8 < MERGE))
    table_ref[:, count:] = onehot(match & (row % 8 >= MERGE))
    for copy in stack:
        copy.wait()


def make_message(slot, saved, projections):
    return pl.pallas_call(
        message_kernel,
        out_shape=(
            jax.ShapeDtypeStruct((SLOTS, SAVED_ROWS, SAVED_WIDE), BF16),
            jax.ShapeDtypeStruct((8 * SLOTS, 2 * MERGE * SLOTS), BF16),
            jax.ShapeDtypeStruct((3 * SHARD, WIDTH), BF16),
        ),
        in_specs=[VMEM] + [HBM] * 4,
        out_specs=(VMEM, VMEM, HBM),
        scratch_shapes=[
            pltpu.VMEM((MERGE * SLOTS, WIDTH), BF16),
            pltpu.SemaphoreType.DMA((4,)),
        ],
        compiler_params=PARAMS,
    )(slot, saved, *projections)


def rows_kernel(early_ref, middle_ref, late_ref, rows_ref, shares_ref, sums):
    used = MERGE * TOKENS
    for j in range(MERGE):
        at = slice(j * WIDTH, (j + 1) * WIDTH)
        to = slice(j * TOKENS, (j + 1) * TOKENS)
        late = late_ref[:, at].astype(F32)
        middle = late + middle_ref[:, at].astype(F32)
        sums[to, 2 * WIDTH : 3 * WIDTH] = late
        sums[to, WIDTH : 2 * WIDTH] = middle
        sums[to, :WIDTH] = middle + early_ref[:, at].astype(F32)
    rows_ref[...] = jnp.zeros_like(rows_ref)
    rows_ref[FIRST : FIRST + used, : 3 * WIDTH] = sums[...].astype(BF16)
    early = sums[:, :WIDTH]
    main = [early[:, d * SHARD : d * SHARD + 128] for d in range(8)]
    rest = [early[:, d * SHARD + 128 : (d + 1) * SHARD] for d in range(8)]
    shares_ref[...] = jnp.concatenate(main + rest, axis=1).astype(BF16)


def make_rows(early, middle, late):
    return pl.pallas_call(
        rows_kernel,
        out_shape=(
            jax.ShapeDtypeStruct((128, 2 * ROWS_HALF), BF16),
            jax.ShapeDtypeStruct((MERGE * TOKENS, WIDTH), BF16),
        ),
        in_specs=[VMEM] * 3,
        out_specs=(VMEM,) * 2,
        scratch_shapes=[pltpu.VMEM((MERGE * TOKENS, 3 * WIDTH), F32)],
        compiler_params=PARAMS,
    )(early, middle, late)


def place_key(column):
    j = sum((column >= k * TOKENS).astype(jnp.int32) for k in range(1, MERGE))
    return column - TOKENS * j + 1 + 32 * j


def pack_kernel(at_ref, arrived_ref, rows_ref, packed_ref):
    arrived = arrived_ref[...].astype(F32).reshape(SLOTS * SAVED_ROWS, SAVED_WIDE).astype(BF16)
    shape = (8 * SLOTS, SLOTS * SAVED_ROWS)
    row, column = iota(shape, 0), iota(shape, 1)
    mine = MERGE * at_ref[2]
    spread = onehot((row // 8 == column // SAVED_ROWS) & (column % SAVED_ROWS == mine))
    asked = matmul(spread, arrived[:, SAVED_WIDE - 128 :])
    row, column = iota((8 * SLOTS, 128), 0), iota((8 * SLOTS, 128), 1)
    inside = (column >= FIRST) & (column < FIRST + MERGE * TOKENS)
    key = place_key(column - FIRST).astype(F32)
    match = inside & (asked + (32 * (row % MERGE)).astype(F32) == key)
    packed = matmul(onehot(match & (row % 8 < MERGE)), rows_ref[:, :ROWS_HALF])
    packed = packed + matmul(onehot(match & (row % 8 >= MERGE)), rows_ref[:, ROWS_HALF:])
    packed_ref[...] = packed.reshape(SLOTS, 8, ROWS_HALF).astype(BF16)


def pack(at, arrived, rows):
    return pl.pallas_call(
        pack_kernel,
        out_shape=jax.ShapeDtypeStruct((SLOTS, 8, ROWS_HALF), BF16),
        in_specs=[SMEM, VMEM, VMEM],
        out_specs=VMEM,
        compiler_params=PARAMS,
    )(at, arrived, rows)


def gradient_kernel(at_ref, arrived_ref, *refs):
    shares, (keep_ref, give_ref, product, terms) = refs[:4], refs[4:]
    x, core, y = at_ref[0], at_ref[1], at_ref[2]
    used = MERGE * TOKENS
    arrived = arrived_ref[...].astype(F32).reshape(SLOTS * SAVED_ROWS, SAVED_WIDE)
    row = iota((SLOTS * SAVED_ROWS, 128), 0)
    behind = (y + 4 - row // MERGE % 4) % 4
    tag = arrived[:, SAVED_WIDE - 128 :] + (32 * (row % MERGE) + 128 * behind).astype(F32)
    column = iota((1, 4 * used), 1)
    block = sum((column >= k * used).astype(jnp.int32) for k in range(1, 4))
    key = (place_key(column - used * block) + 128 * block).astype(F32)
    match = onehot(tag[:, 127:128] == key)
    saved = matmul_tn(arrived.astype(BF16), match)[:QUARTER].astype(BF16)
    product[...] = matmul(saved, jnp.concatenate([ref[...] for ref in shares], axis=0))

    line = iota((1, QUARTER), 1).astype(F32)
    block = quotient(line, OWN)
    inside = line - OWN * block
    group = quotient(inside, 8)
    to = 8 * REST * (inside - 8 * group) + REST * block + group
    order = onehot(iota((8 * 8 * REST, QUARTER), 0).astype(F32) == to)
    rest = matmul(order, product[:, 8 * 128 :].astype(BF16))
    at = iota((8 * REST, 128), 1) // 16
    fill = jnp.zeros((TERM_ROWS - OWN - REST, 128), F32)
    for d in range(8):
        folded = jnp.zeros((8 * REST, 128), F32)
        for b in range(8):
            part = rest[8 * REST * b : 8 * REST * (b + 1)]
            if b != d:
                part = pltpu.roll(part, 16 * (b - d) % 128, 1)
            folded = jnp.where(at == b, part, folded)
        step = lax.rem(d // 2 + 4 - x, 4)
        side = lax.rem(d % 2 + core, 2)
        for z in range(8):
            main = product[OWN * z : OWN * (z + 1), 128 * d : 128 * (d + 1)]
            parts = [main, folded[REST * z : REST * (z + 1)], fill]
            terms[side, step, z] = jnp.concatenate(parts, axis=0)
    keep_ref[...] = terms[0]
    give_ref[...] = terms[1].astype(BF16)


def gradient(at, arrived, shares):
    shape = (4, 8, TERM_ROWS, 128)
    return pl.pallas_call(
        gradient_kernel,
        out_shape=(jax.ShapeDtypeStruct(shape, F32), jax.ShapeDtypeStruct(shape, BF16)),
        in_specs=[SMEM] + [VMEM] * 5,
        out_specs=(VMEM,) * 2,
        scratch_shapes=[pltpu.VMEM((QUARTER, WIDTH), F32), pltpu.VMEM((2, *shape), F32)],
        compiler_params=PARAMS,
    )(at, arrived, *shares)


def core_kernel(keep_ref, given_ref, *out_refs):
    for step, out in enumerate(out_refs):
        out[...] = (keep_ref[step] + given_ref[step].astype(F32)).astype(out.dtype)


def sum_core(keep, given):
    shape = keep.shape[1:]
    return pl.pallas_call(
        core_kernel,
        out_shape=[jax.ShapeDtypeStruct(shape, F32)] + [jax.ShapeDtypeStruct(shape, BF16)] * 3,
        in_specs=[VMEM] * 2,
        out_specs=[VMEM] * 4,
        compiler_params=PARAMS,
    )(keep, given)


def sum_kernel(own_ref, first, second, third, out_ref):
    total = own_ref[...]
    for ref in (first, second, third):
        total = total + ref[...].astype(F32)
    out_ref[...] = total.astype(BF16)


def sum_x(own, parts):
    return pl.pallas_call(
        sum_kernel,
        out_shape=jax.ShapeDtypeStruct(own.shape, BF16),
        in_specs=[VMEM] * 4,
        out_specs=VMEM,
        compiler_params=PARAMS,
    )(own, *parts)


def total_kernel(terms_ref, out_ref):
    total = terms_ref[0].astype(F32)
    for c in range(1, 8):
        total = total + terms_ref[c].astype(F32)
    rest = jnp.concatenate(
        [jnp.broadcast_to(total[OWN + a : OWN + a + 1], (8, 128)) for a in range(REST)], axis=0
    )[:OWN]
    line, column = iota((OWN, 128), 0), iota((OWN, 128), 1)
    rest = jnp.where(line % 8 == column // 16, rest, 0.0)
    for shift in (64, 32, 16):
        rest = rest + pltpu.roll(rest, shift, 1)
    out_ref[:, :128] = total[:OWN]
    out_ref[:, 128:] = rest[:, : SHARD - 128]


def add_up(terms):
    return pl.pallas_call(
        total_kernel,
        out_shape=jax.ShapeDtypeStruct((OWN, SHARD), F32),
        in_specs=[VMEM],
        out_specs=VMEM,
        compiler_params=PARAMS,
    )(terms)


def context_kernel(cut, at_ref, table_ref, landed_ref, *refs):
    pieces = refs[:10]
    early_out, middle_out, late_out, stream_out, weight, sem = refs[10:]
    x, core = at_ref[0], at_ref[1]
    copies = ([], [], [])

    def put(ref, first, rows, m, inside, of_x, of_core):
        base = pl.multiple_of((2 * of_x + of_core) * SHARD + inside, 16)
        copies[m].append(
            pltpu.make_async_copy(
                ref.at[pl.ds(first, rows)], weight.at[m, pl.ds(base, rows)], sem.at[m]
            )
        )

    for index, of_core in ((0, core), (5, 1 - core)):
        for k, step in enumerate((0, 3, 1)):
            for m in range(3):
                put(pieces[index + k], m * SHARD, SHARD, m, 0, lax.rem(x + step, 4), of_core)
        of_x = lax.rem(x + 2, 4)
        for ref, start, stop in ((pieces[index + 3], 0, cut), (pieces[index + 4], cut, 3 * SHARD)):
            for m in range(3):
                low, high = max(start, m * SHARD), min(stop, (m + 1) * SHARD)
                if low < high:
                    put(ref, low - start, high - low, m, low - m * SHARD, of_x, of_core)
    for m in range(3):
        for copy in copies[m]:
            copy.start()
    landed = landed_ref[...].astype(F32).reshape(8 * SLOTS, ROWS_HALF).astype(BF16)
    placed = matmul_tn(table_ref[...], landed).astype(BF16)
    half = MERGE * SLOTS
    placed = jnp.concatenate([placed[:half], placed[half:, : 3 * WIDTH - ROWS_HALF]], axis=1)
    stream_out[...] = placed[:, :WIDTH]
    for m, out in enumerate((early_out, middle_out, late_out)):
        for copy in copies[m]:
            copy.wait()
        out[...] = lax.dot_general(
            placed[:, m * WIDTH : (m + 1) * WIDTH],
            weight[m],
            (((1,), (1,)), ((), ())),
            preferred_element_type=F32,
        ).astype(BF16)


def contexts(at, table, landed, pieces, cut):
    rows = MERGE * SLOTS
    out = jax.ShapeDtypeStruct((rows, WIDTH), BF16)
    return pl.pallas_call(
        lambda *refs: context_kernel(cut, *refs),
        out_shape=(out,) * 4,
        in_specs=[SMEM, VMEM, VMEM] + [HBM] * 10,
        out_specs=(VMEM,) * 4,
        scratch_shapes=[
            pltpu.VMEM((3, WIDTH, WIDTH), BF16),
            pltpu.SemaphoreType.DMA((3,)),
        ],
        compiler_params=PARAMS,
        cost_estimate=pl.CostEstimate(
            flops=6 * rows * WIDTH * WIDTH, bytes_accessed=6 * WIDTH * WIDTH, transcendentals=0
        ),
    )(at, table, landed, *pieces)


def local(
    injected_early,
    injected_middle,
    injected_late,
    slot_source,
    saved_early,
    projection_early,
    projection_middle,
    projection_late,
):
    at = jnp.stack([lax.axis_index(name) for name in ("x", "core", "y")]).astype(jnp.int32)

    projections = (projection_early, projection_middle, projection_late)
    message, table, stacked = make_message(slot_source, saved_early[0], projections)
    arrived = lax.all_to_all(message, CTX, 0, 0, tiled=True)

    cut = 224
    from_left, from_right = over_x(stacked, 1), over_x(stacked, 3)
    rows, share = make_rows(injected_early[0], injected_middle[0], injected_late[0])
    shares = [share] + [over_y(share, step) for step in (1, 2, 3)]
    arrived, from_left, from_right, shares = lax.optimization_barrier(
        (arrived, from_left, from_right, shares)
    )

    landed = lax.all_to_all(pack(at, arrived, rows), CTX, 0, 0, tiled=True)

    far_left, far_right = over_x(from_left[:cut], 1), over_x(from_right[cut:], 3)

    keep, give = gradient(at, arrived, shares)
    given = over_core(give)
    given, far_left, far_right = lax.optimization_barrier((given, far_left, far_right))
    mine, *parts = sum_core(keep, given)
    parts = [over_x(part, step) for step, part in zip((1, 2, 3), parts)]
    terms = sum_x(mine, parts)
    terms, landed = lax.optimization_barrier((terms, landed))
    weights = add_up(lax.all_to_all(terms, "z", 0, 0, tiled=True))

    pieces = (stacked, from_left, from_right, far_left, far_right)
    pieces = pieces + tuple(over_core(piece) for piece in pieces)
    context_early, context_middle, context_late, stream = contexts(at, table, landed, pieces, cut)
    return context_early[None], context_middle[None], context_late[None], stream[None], weights


def solution(mesh):
    fine = Mesh(mesh.devices.reshape(4, 2, 8, 4), ("x", "core", "z", "y"))
    rows = P(DP, CTX, None)
    return jax.shard_map(
        local,
        mesh=fine,
        in_specs=(rows, rows, rows, P(DP, CTX), rows, P(DP, None), P(DP, None), P(DP, None)),
        out_specs=(rows, rows, rows, rows, P(CTX, DP)),
        check_vma=False,
    )
```

```python
import jax
import jax.numpy as jnp
from jax import lax
from jax.experimental import pallas as pl
from jax.experimental.pallas import tpu as pltpu
from jax.sharding import Mesh, PartitionSpec as P

DP = ("x", "core")
CTX = ("z", "y")
BF16 = jnp.bfloat16
F32 = jnp.float32
VMEM = pl.BlockSpec(memory_space=pltpu.VMEM)
SMEM = pl.BlockSpec(memory_space=pltpu.SMEM)
HBM = pl.BlockSpec(memory_space=pltpu.HBM)
PARAMS = pltpu.CompilerParams(vmem_limit_bytes=16 << 20)


def cost(mib):
    return pl.CostEstimate(flops=0, bytes_accessed=mib << 20, transcendentals=0)


WIDTH = 1152
MERGE = 4
TOKENS = 20
SLOTS = 32
SHARD = 144
CUT = 224
OWN = 36
QUARTER = 288
SAVED_WIDE = 384
SAVED_ROWS = 16
FIRST = 32
ROWS_HALF = 1792
TERM_ROWS = 48
REST = 5


def over_x(array, step):
    return lax.ppermute(array, "x", [(i, (i + step) % 4) for i in range(4)])


def over_y(array, step):
    return lax.ppermute(array, "y", [(i, (i + step) % 4) for i in range(4)])


def over_core(array):
    return lax.ppermute(array, "core", [(0, 1), (1, 0)])


def iota(shape, dim):
    return lax.broadcasted_iota(jnp.int32, shape, dim)


def onehot(condition):
    return jnp.where(condition, 1.0, 0.0).astype(BF16)


def matmul(a, b):
    return jnp.dot(a, b, preferred_element_type=F32)


def matmul_tn(a, b):
    return lax.dot_general(a, b, (((0,), (0,)), ((), ())), preferred_element_type=F32)


def quotient(value, by):
    return jnp.floor((value + 0.5) * (1.0 / by))


def first_kernel(
    slot_ref,
    *refs,
):
    inputs, outputs, (saved_ref, rows_in, sums, sem) = refs[:7], refs[7:12], refs[12:]
    message_ref, table_ref, stacked_ref, rows_ref, shares_ref = outputs
    fetch_saved = pltpu.make_async_copy(inputs[0], saved_ref, sem.at[0])
    fetch_rows = [
        pltpu.make_async_copy(ref, rows_in.at[m], sem.at[1 + m])
        for m, ref in enumerate(inputs[1:4])
    ]
    stack = [
        pltpu.make_async_copy(ref, stacked_ref.at[pl.ds(m * SHARD, SHARD)], sem.at[4 + m])
        for m, ref in enumerate(inputs[4:7])
    ]
    for copy in (fetch_saved, *fetch_rows, *stack):
        copy.start()

    source = slot_ref[...].astype(F32)
    sender = quotient(source, TOKENS)
    place = source - TOKENS * sender
    both = jnp.where(iota((8, SLOTS), 0) == 0, sender, place).astype(BF16)
    repeat = onehot(iota((SLOTS, SLOTS * MERGE), 1) // MERGE == iota((SLOTS, SLOTS * MERGE), 0))
    wide = matmul(both, repeat)
    sender, place = wide[0:1], wide[1:2]
    count = MERGE * SLOTS
    row, column = iota((2 * count, count), 0), iota((2 * count, count), 1)
    match = (sender == (row // 8).astype(F32)) & (row % MERGE == column % MERGE)
    table_ref[:, :count] = onehot(match & (row % 8 < MERGE))
    table_ref[:, count:] = onehot(match & (row % 8 >= MERGE))
    row, column = iota((count, count), 0), iota((count, count), 1)
    match = (sender == (row // MERGE).astype(F32)) & (row % MERGE == column % MERGE)
    tag = jnp.sum(jnp.where(match, place + 1.0, 0.0), axis=1, keepdims=True)
    tag = jnp.broadcast_to(tag, (count, SAVED_WIDE - QUARTER))
    match = onehot(match)
    fetch_saved.wait()
    sorted_rows = matmul(match, saved_ref[...])
    for y in range(4):
        blocks = [sorted_rows[:, OWN * c : OWN * (c + 1)] for c in range(y, SLOTS, 4)]
        message = jnp.concatenate(blocks + [tag], axis=1).astype(BF16)
        for z in range(8):
            message_ref[4 * z + y] = message[SAVED_ROWS * z : SAVED_ROWS * (z + 1)]

    used = MERGE * TOKENS
    rows_ref[...] = jnp.zeros_like(rows_ref)
    for copy in fetch_rows:
        copy.wait()
    for j in range(MERGE):
        at = slice(j * WIDTH, (j + 1) * WIDTH)
        to = slice(j * TOKENS, (j + 1) * TOKENS)
        late = rows_in[2, :, at].astype(F32)
        middle = late + rows_in[1, :, at].astype(F32)
        sums[to, 2 * WIDTH : 3 * WIDTH] = late
        sums[to, WIDTH : 2 * WIDTH] = middle
        sums[to, :WIDTH] = middle + rows_in[0, :, at].astype(F32)
    rows_ref[FIRST : FIRST + used, : 3 * WIDTH] = sums[...].astype(BF16)
    early = sums[:, :WIDTH]
    main = [early[:, d * SHARD : d * SHARD + 128] for d in range(8)]
    rest = [early[:, d * SHARD + 128 : (d + 1) * SHARD] for d in range(8)]
    shares_ref[...] = jnp.concatenate(main + rest, axis=1).astype(BF16)
    for copy in stack:
        copy.wait()


def first(slot, saved, injected, projections):
    return pl.pallas_call(
        first_kernel,
        out_shape=(
            jax.ShapeDtypeStruct((SLOTS, SAVED_ROWS, SAVED_WIDE), BF16),
            jax.ShapeDtypeStruct((8 * SLOTS, 2 * MERGE * SLOTS), BF16),
            jax.ShapeDtypeStruct((3 * SHARD, WIDTH), BF16),
            jax.ShapeDtypeStruct((128, 2 * ROWS_HALF), BF16),
            jax.ShapeDtypeStruct((MERGE * TOKENS, WIDTH), BF16),
        ),
        in_specs=[VMEM] + [HBM] * 7,
        out_specs=(VMEM,) * 5,
        scratch_shapes=[
            pltpu.VMEM((MERGE * SLOTS, WIDTH), BF16),
            pltpu.VMEM((3, TOKENS, MERGE * WIDTH), BF16),
            pltpu.VMEM((MERGE * TOKENS, 3 * WIDTH), F32),
            pltpu.SemaphoreType.DMA((7,)),
        ],
        cost_estimate=cost(8),
    )(slot, saved, *injected, *projections)


def place_key(column):
    j = sum((column >= k * TOKENS).astype(jnp.int32) for k in range(1, MERGE))
    return column - TOKENS * j + 1 + 32 * j


def pack_kernel(at_ref, arrived_ref, rows_ref, packed_ref):
    arrived = arrived_ref[...].astype(F32).reshape(SLOTS * SAVED_ROWS, SAVED_WIDE).astype(BF16)
    shape = (8 * SLOTS, SLOTS * SAVED_ROWS)
    row, column = iota(shape, 0), iota(shape, 1)
    mine = MERGE * at_ref[2]
    spread = onehot((row // 8 == column // SAVED_ROWS) & (column % SAVED_ROWS == mine))
    asked = matmul(spread, arrived[:, SAVED_WIDE - 128 :])
    row, column = iota((8 * SLOTS, 128), 0), iota((8 * SLOTS, 128), 1)
    inside = (column >= FIRST) & (column < FIRST + MERGE * TOKENS)
    key = place_key(column - FIRST).astype(F32)
    match = inside & (asked + (32 * (row % MERGE)).astype(F32) == key)
    packed = matmul(onehot(match & (row % 8 < MERGE)), rows_ref[:, :ROWS_HALF])
    packed = packed + matmul(onehot(match & (row % 8 >= MERGE)), rows_ref[:, ROWS_HALF:])
    packed_ref[...] = packed.reshape(SLOTS, 8, ROWS_HALF).astype(BF16)


def pack(at, arrived, rows):
    return pl.pallas_call(
        pack_kernel,
        out_shape=jax.ShapeDtypeStruct((SLOTS, 8, ROWS_HALF), BF16),
        in_specs=[SMEM, VMEM, VMEM],
        out_specs=VMEM,
        compiler_params=PARAMS,
        cost_estimate=cost(40),
    )(at, arrived, rows)


def gradient_kernel(at_ref, arrived_ref, *refs):
    shares, (keep_ref, give_ref, product, terms) = refs[:4], refs[4:]
    x, core, y = at_ref[0], at_ref[1], at_ref[2]
    used = MERGE * TOKENS
    arrived = arrived_ref[...].astype(F32).reshape(SLOTS * SAVED_ROWS, SAVED_WIDE)
    row = iota((SLOTS * SAVED_ROWS, 128), 0)
    behind = (y + 4 - row // MERGE % 4) % 4
    tag = arrived[:, SAVED_WIDE - 128 :] + (32 * (row % MERGE) + 128 * behind).astype(F32)
    column = iota((1, 4 * used), 1)
    block = sum((column >= k * used).astype(jnp.int32) for k in range(1, 4))
    key = (place_key(column - used * block) + 128 * block).astype(F32)
    match = onehot(tag[:, 127:128] == key)
    saved = matmul_tn(arrived.astype(BF16), match)[:QUARTER].astype(BF16)
    product[...] = matmul(saved, jnp.concatenate([ref[...] for ref in shares], axis=0))

    line = iota((1, QUARTER), 1).astype(F32)
    block = quotient(line, OWN)
    inside = line - OWN * block
    group = quotient(inside, 8)
    to = 8 * REST * (inside - 8 * group) + REST * block + group
    order = onehot(iota((8 * 8 * REST, QUARTER), 0).astype(F32) == to)
    rest = matmul(order, product[:, 8 * 128 :].astype(BF16))
    at = iota((8 * REST, 128), 1) // 16
    fill = jnp.zeros((TERM_ROWS - OWN - REST, 128), F32)
    for d in range(8):
        folded = jnp.zeros((8 * REST, 128), F32)
        for b in range(8):
            part = rest[8 * REST * b : 8 * REST * (b + 1)]
            if b != d:
                part = pltpu.roll(part, 16 * (b - d) % 128, 1)
            folded = jnp.where(at == b, part, folded)
        step = lax.rem(d // 2 + 4 - x, 4)
        side = lax.rem(d % 2 + core, 2)
        for z in range(8):
            main = product[OWN * z : OWN * (z + 1), 128 * d : 128 * (d + 1)]
            parts = [main, folded[REST * z : REST * (z + 1)], fill]
            terms[side, step, z] = jnp.concatenate(parts, axis=0)
    keep_ref[...] = terms[0]
    give_ref[...] = terms[1].astype(BF16)


def gradient(at, arrived, shares):
    shape = (4, 8, TERM_ROWS, 128)
    return pl.pallas_call(
        gradient_kernel,
        out_shape=(jax.ShapeDtypeStruct(shape, F32), jax.ShapeDtypeStruct(shape, BF16)),
        in_specs=[SMEM] + [VMEM] * 5,
        out_specs=(VMEM,) * 2,
        scratch_shapes=[pltpu.VMEM((QUARTER, WIDTH), F32), pltpu.VMEM((2, *shape), F32)],
        compiler_params=PARAMS,
        cost_estimate=cost(40),
    )(at, arrived, *shares)


def core_kernel(keep_ref, given_ref, *out_refs):
    for step, out in enumerate(out_refs):
        out[...] = (keep_ref[step] + given_ref[step].astype(F32)).astype(out.dtype)


def sum_core(keep, given):
    shape = keep.shape[1:]
    return pl.pallas_call(
        core_kernel,
        out_shape=[jax.ShapeDtypeStruct(shape, F32)] + [jax.ShapeDtypeStruct(shape, BF16)] * 3,
        in_specs=[VMEM] * 2,
        out_specs=[VMEM] * 4,
        compiler_params=PARAMS,
    )(keep, given)


def sum_kernel(own_ref, first, second, third, out_ref):
    total = own_ref[...]
    for ref in (first, second, third):
        total = total + ref[...].astype(F32)
    out_ref[...] = total.astype(BF16)


def sum_x(own, parts):
    return pl.pallas_call(
        sum_kernel,
        out_shape=jax.ShapeDtypeStruct(own.shape, BF16),
        in_specs=[VMEM] * 4,
        out_specs=VMEM,
        compiler_params=PARAMS,
    )(own, *parts)


def total_kernel(terms_ref, out_ref):
    total = terms_ref[0].astype(F32)
    for c in range(1, 8):
        total = total + terms_ref[c].astype(F32)
    rest = jnp.concatenate(
        [jnp.broadcast_to(total[OWN + a : OWN + a + 1], (8, 128)) for a in range(REST)], axis=0
    )[:OWN]
    line, column = iota((OWN, 128), 0), iota((OWN, 128), 1)
    rest = jnp.where(line % 8 == column // 16, rest, 0.0)
    for shift in (64, 32, 16):
        rest = rest + pltpu.roll(rest, shift, 1)
    out_ref[:, :128] = total[:OWN]
    out_ref[:, 128:] = rest[:, : SHARD - 128]


def add_up(terms):
    return pl.pallas_call(
        total_kernel,
        out_shape=jax.ShapeDtypeStruct((OWN, SHARD), F32),
        in_specs=[VMEM],
        out_specs=VMEM,
        compiler_params=PARAMS,
    )(terms)


def context_kernel(at_ref, table_ref, landed_ref, *refs):
    pieces, outs, (stream_out, weight, sem) = refs[:10], refs[10:13], refs[13:]
    x, core = at_ref[0], at_ref[1]
    copies = []
    for m in range(3):
        for k, ref in enumerate(pieces):
            of_core = core if k < 5 else 1 - core
            of_x = lax.rem(x + (0, 3, 1, 2, 2)[k % 5], 4)
            start = CUT if k % 5 == 4 else 0
            stop = CUT if k % 5 == 3 else 3 * SHARD
            low, high = max(start, m * SHARD), min(stop, (m + 1) * SHARD)
            if low < high:
                base = pl.multiple_of((2 * of_x + of_core) * SHARD + low - m * SHARD, 16)
                from_ref = ref.at[pl.ds(low - start, high - low)]
                to_ref = weight.at[m, pl.ds(base, high - low)]
                copies.append((m, pltpu.make_async_copy(from_ref, to_ref, sem.at[m])))
    for _, copy in copies:
        copy.start()
    landed = landed_ref[...].astype(F32).reshape(8 * SLOTS, ROWS_HALF).astype(BF16)
    placed = matmul_tn(table_ref[...], landed).astype(BF16)
    half = MERGE * SLOTS
    placed = jnp.concatenate([placed[:half], placed[half:, : 3 * WIDTH - ROWS_HALF]], axis=1)
    stream_out[...] = placed[:, :WIDTH]
    for m, out in enumerate(outs):
        for of_m, copy in copies:
            if of_m == m:
                copy.wait()
        out[...] = lax.dot_general(
            placed[:, m * WIDTH : (m + 1) * WIDTH],
            weight[m],
            (((1,), (1,)), ((), ())),
            preferred_element_type=F32,
        ).astype(BF16)


def contexts(at, table, landed, pieces):
    out = jax.ShapeDtypeStruct((MERGE * SLOTS, WIDTH), BF16)
    return pl.pallas_call(
        context_kernel,
        out_shape=(out,) * 4,
        in_specs=[SMEM, VMEM, VMEM] + [HBM] * 10,
        out_specs=(VMEM,) * 4,
        scratch_shapes=[
            pltpu.VMEM((3, WIDTH, WIDTH), BF16),
            pltpu.SemaphoreType.DMA((3,)),
        ],
        compiler_params=pltpu.CompilerParams(vmem_limit_bytes=58 << 20),
        cost_estimate=cost(24),
    )(at, table, landed, *pieces)


def local(
    injected_early,
    injected_middle,
    injected_late,
    slot_source,
    saved_early,
    projection_early,
    projection_middle,
    projection_late,
):
    at = jnp.stack([lax.axis_index(name) for name in ("x", "core", "y")]).astype(jnp.int32)

    message, table, stacked, rows, share = first(
        slot_source,
        saved_early[0],
        (injected_early[0], injected_middle[0], injected_late[0]),
        (projection_early, projection_middle, projection_late),
    )
    arrived = lax.all_to_all(message, CTX, 0, 0, tiled=True)

    from_left, from_right = over_x(stacked, 1), over_x(stacked, 3)
    shares = [share] + [over_y(share, step) for step in (1, 2, 3)]
    once_more = from_left[:CUT], from_right[CUT:]
    arrived, shares, from_left, from_right, once_more = lax.optimization_barrier(
        (arrived, shares, from_left, from_right, once_more)
    )

    landed = lax.all_to_all(pack(at, arrived, rows), CTX, 0, 0, tiled=True)

    far = over_x(once_more[0], 1), over_x(once_more[1], 3)
    keep, give = gradient(at, arrived, shares)
    mine, *parts = sum_core(keep, over_core(give))
    parts = [over_x(part, step) for step, part in zip((1, 2, 3), parts)]
    parts, far = lax.optimization_barrier((parts, far))
    terms = sum_x(mine, parts)

    pieces = (stacked, from_left, from_right, *far)
    terms, pieces = lax.optimization_barrier((terms, pieces))
    pieces = pieces + tuple(over_core(piece) for piece in pieces)
    terms, landed = lax.optimization_barrier((terms, landed))
    weights = add_up(lax.all_to_all(terms, "z", 0, 0, tiled=True))
    context_early, context_middle, context_late, stream = contexts(at, table, landed, pieces)
    return context_early[None], context_middle[None], context_late[None], stream[None], weights


def solution(mesh):
    fine = Mesh(mesh.devices.reshape(4, 2, 8, 4), ("x", "core", "z", "y"))
    rows = P(DP, CTX, None)
    return jax.shard_map(
        local,
        mesh=fine,
        in_specs=(rows, rows, rows, P(DP, CTX), rows, P(DP, None), P(DP, None), P(DP, None)),
        out_specs=(rows, rows, rows, rows, P(CTX, DP)),
        check_vma=False,
    )
```

```python
import jax
import jax.numpy as jnp
from jax import lax
from jax.experimental import pallas as pl
from jax.experimental.pallas import tpu as pltpu
from jax.sharding import Mesh, PartitionSpec as P

DP = ("x", "core")
CTX = ("z", "y")
BF16 = jnp.bfloat16
F32 = jnp.float32
VMEM = pl.BlockSpec(memory_space=pltpu.VMEM)
SMEM = pl.BlockSpec(memory_space=pltpu.SMEM)
HBM = pl.BlockSpec(memory_space=pltpu.HBM)
PARAMS = pltpu.CompilerParams(vmem_limit_bytes=16 << 20)


def cost(mib):
    return pl.CostEstimate(flops=0, bytes_accessed=mib << 20, transcendentals=0)


WIDTH = 1152
MERGE = 4
TOKENS = 20
SLOTS = 32
SHARD = 144
CUT = 224
OWN = 36
QUARTER = 288
SAVED_WIDE = 384
SAVED_ROWS = 16
FIRST = 32
ROWS_HALF = 1792
TERM_ROWS = 48
REST = 5


def over_x(array, step):
    return lax.ppermute(array, "x", [(i, (i + step) % 4) for i in range(4)])


def over_y(array, step):
    return lax.ppermute(array, "y", [(i, (i + step) % 4) for i in range(4)])


def over_core(array):
    return lax.ppermute(array, "core", [(0, 1), (1, 0)])


def iota(shape, dim):
    return lax.broadcasted_iota(jnp.int32, shape, dim)


def onehot(condition):
    return jnp.where(condition, 1.0, 0.0).astype(BF16)


def matmul(a, b):
    return jnp.dot(a, b, preferred_element_type=F32)


def matmul_tn(a, b):
    return lax.dot_general(a, b, (((0,), (0,)), ((), ())), preferred_element_type=F32)


def quotient(value, by):
    return jnp.floor((value + 0.5) * (1.0 / by))


def first_kernel(slot_hbm, saved_hbm, message_ref, table_ref, slot_ref, saved_ref, sem):
    fetch_slot = pltpu.make_async_copy(slot_hbm, slot_ref, sem.at[0])
    fetch_saved = pltpu.make_async_copy(saved_hbm, saved_ref, sem.at[1])
    fetch_slot.start()
    fetch_saved.start()
    fetch_slot.wait()

    source = slot_ref[...].astype(F32)
    sender = quotient(source, TOKENS)
    place = source - TOKENS * sender
    both = jnp.where(iota((8, SLOTS), 0) == 0, sender, place).astype(BF16)
    repeat = onehot(iota((SLOTS, SLOTS * MERGE), 1) // MERGE == iota((SLOTS, SLOTS * MERGE), 0))
    wide = matmul(both, repeat)
    sender, place = wide[0:1], wide[1:2]
    count = MERGE * SLOTS
    row, column = iota((2 * count, count), 0), iota((2 * count, count), 1)
    match = (sender == (row // 8).astype(F32)) & (row % MERGE == column % MERGE)
    table_ref[:, :count] = onehot(match & (row % 8 < MERGE))
    table_ref[:, count:] = onehot(match & (row % 8 >= MERGE))
    row, column = iota((count, count), 0), iota((count, count), 1)
    match = (sender == (row // MERGE).astype(F32)) & (row % MERGE == column % MERGE)
    tag = jnp.sum(jnp.where(match, place + 1.0, 0.0), axis=1, keepdims=True)
    tag = jnp.broadcast_to(tag, (count, SAVED_WIDE - QUARTER))
    match = onehot(match)
    fetch_saved.wait()
    sorted_rows = matmul(match, saved_ref[...])
    for y in range(4):
        blocks = [sorted_rows[:, OWN * c : OWN * (c + 1)] for c in range(y, SLOTS, 4)]
        message = jnp.concatenate(blocks + [tag], axis=1).astype(BF16)
        for z in range(8):
            message_ref[4 * z + y] = message[SAVED_ROWS * z : SAVED_ROWS * (z + 1)]


def first(slot, saved):
    return pl.pallas_call(
        first_kernel,
        out_shape=(
            jax.ShapeDtypeStruct((SLOTS, SAVED_ROWS, SAVED_WIDE), BF16),
            jax.ShapeDtypeStruct((8 * SLOTS, 2 * MERGE * SLOTS), BF16),
        ),
        in_specs=[HBM] * 2,
        out_specs=(VMEM,) * 2,
        scratch_shapes=[
            pltpu.VMEM(slot.shape, jnp.int32),
            pltpu.VMEM(saved.shape, BF16),
            pltpu.SemaphoreType.DMA((2,)),
        ],
        compiler_params=pltpu.CompilerParams(vmem_limit_bytes=58 << 20),
        cost_estimate=cost(8),
    )(slot, saved)


def stack_kernel(early_ref, middle_ref, late_ref, stacked_ref):
    for m, ref in enumerate((early_ref, middle_ref, late_ref)):
        stacked_ref[m * SHARD : (m + 1) * SHARD] = ref[...]


def stack(projections):
    return pl.pallas_call(
        stack_kernel,
        out_shape=jax.ShapeDtypeStruct((3 * SHARD, WIDTH), BF16),
        in_specs=[VMEM] * 3,
        out_specs=VMEM,
        compiler_params=pltpu.CompilerParams(vmem_limit_bytes=8 << 20),
        cost_estimate=cost(4),
    )(*projections)


def add_down(refs, sums, at):
    early_ref, middle_ref, late_ref = refs
    for j in range(MERGE):
        columns = slice(j * WIDTH, (j + 1) * WIDTH)
        to = slice(j * TOKENS, (j + 1) * TOKENS)
        late = late_ref[:, columns].astype(F32)
        middle = late + middle_ref[:, columns].astype(F32)
        sums[to, :WIDTH] = middle + early_ref[:, columns].astype(F32)
        if at > WIDTH:
            sums[to, 2 * WIDTH :] = late
            sums[to, WIDTH : 2 * WIDTH] = middle


def share_kernel(early_ref, middle_ref, late_ref, shares_ref, sums):
    add_down((early_ref, middle_ref, late_ref), sums, WIDTH)
    early = sums[...]
    main = [early[:, d * SHARD : d * SHARD + 128] for d in range(8)]
    rest = [early[:, d * SHARD + 128 : (d + 1) * SHARD] for d in range(8)]
    shares_ref[...] = jnp.concatenate(main + rest, axis=1).astype(BF16)


def rows_kernel(early_ref, middle_ref, late_ref, rows_ref, sums):
    used = MERGE * TOKENS
    add_down((early_ref, middle_ref, late_ref), sums, 3 * WIDTH)
    rows_ref[...] = jnp.zeros_like(rows_ref)
    rows_ref[FIRST : FIRST + used, : 3 * WIDTH] = sums[...].astype(BF16)


def from_injected(kernel, injected, shape, width):
    return pl.pallas_call(
        kernel,
        out_shape=jax.ShapeDtypeStruct(shape, BF16),
        in_specs=[VMEM] * 3,
        out_specs=VMEM,
        scratch_shapes=[pltpu.VMEM((MERGE * TOKENS, width), F32)],
        compiler_params=PARAMS,
        cost_estimate=cost(4),
    )(*injected)


def place_key(column):
    j = sum((column >= k * TOKENS).astype(jnp.int32) for k in range(1, MERGE))
    return column - TOKENS * j + 1 + 32 * j


def pack_kernel(at_ref, arrived_ref, rows_ref, packed_ref):
    arrived = arrived_ref[...].astype(F32).reshape(SLOTS * SAVED_ROWS, SAVED_WIDE).astype(BF16)
    shape = (8 * SLOTS, SLOTS * SAVED_ROWS)
    row, column = iota(shape, 0), iota(shape, 1)
    mine = MERGE * at_ref[2]
    spread = onehot((row // 8 == column // SAVED_ROWS) & (column % SAVED_ROWS == mine))
    asked = matmul(spread, arrived[:, SAVED_WIDE - 128 :])
    row, column = iota((8 * SLOTS, 128), 0), iota((8 * SLOTS, 128), 1)
    inside = (column >= FIRST) & (column < FIRST + MERGE * TOKENS)
    key = place_key(column - FIRST).astype(F32)
    match = inside & (asked + (32 * (row % MERGE)).astype(F32) == key)
    packed = matmul(onehot(match & (row % 8 < MERGE)), rows_ref[:, :ROWS_HALF])
    packed = packed + matmul(onehot(match & (row % 8 >= MERGE)), rows_ref[:, ROWS_HALF:])
    packed_ref[...] = packed.reshape(SLOTS, 8, ROWS_HALF).astype(BF16)


def pack(at, arrived, rows):
    return pl.pallas_call(
        pack_kernel,
        out_shape=jax.ShapeDtypeStruct((SLOTS, 8, ROWS_HALF), BF16),
        in_specs=[SMEM, VMEM, VMEM],
        out_specs=VMEM,
        compiler_params=PARAMS,
        cost_estimate=cost(40),
    )(at, arrived, rows)


def gradient_kernel(at_ref, arrived_ref, *refs):
    shares, (keep_ref, give_ref, product, terms) = refs[:4], refs[4:]
    x, core, y = at_ref[0], at_ref[1], at_ref[2]
    used = MERGE * TOKENS
    arrived = arrived_ref[...].astype(F32).reshape(SLOTS * SAVED_ROWS, SAVED_WIDE)
    row = iota((SLOTS * SAVED_ROWS, 128), 0)
    behind = (y + 4 - row // MERGE % 4) % 4
    tag = arrived[:, SAVED_WIDE - 128 :] + (32 * (row % MERGE) + 128 * behind).astype(F32)
    column = iota((1, 4 * used), 1)
    block = sum((column >= k * used).astype(jnp.int32) for k in range(1, 4))
    key = (place_key(column - used * block) + 128 * block).astype(F32)
    match = onehot(tag[:, 127:128] == key)
    saved = matmul_tn(arrived.astype(BF16), match)[:QUARTER].astype(BF16)
    product[...] = matmul(saved, jnp.concatenate([ref[...] for ref in shares], axis=0))

    line = iota((1, QUARTER), 1).astype(F32)
    block = quotient(line, OWN)
    inside = line - OWN * block
    group = quotient(inside, 8)
    to = 8 * REST * (inside - 8 * group) + REST * block + group
    order = onehot(iota((8 * 8 * REST, QUARTER), 0).astype(F32) == to)
    rest = matmul(order, product[:, 8 * 128 :].astype(BF16))
    at = iota((8 * REST, 128), 1) // 16
    fill = jnp.zeros((TERM_ROWS - OWN - REST, 128), F32)
    for d in range(8):
        folded = jnp.zeros((8 * REST, 128), F32)
        for b in range(8):
            part = rest[8 * REST * b : 8 * REST * (b + 1)]
            if b != d:
                part = pltpu.roll(part, 16 * (b - d) % 128, 1)
            folded = jnp.where(at == b, part, folded)
        step = lax.rem(d // 2 + 4 - x, 4)
        side = lax.rem(d % 2 + core, 2)
        for z in range(8):
            main = product[OWN * z : OWN * (z + 1), 128 * d : 128 * (d + 1)]
            parts = [main, folded[REST * z : REST * (z + 1)], fill]
            terms[side, step, z] = jnp.concatenate(parts, axis=0)
    keep_ref[...] = terms[0]
    give_ref[...] = terms[1].astype(BF16)


def gradient(at, arrived, shares):
    shape = (4, 8, TERM_ROWS, 128)
    return pl.pallas_call(
        gradient_kernel,
        out_shape=(jax.ShapeDtypeStruct(shape, F32), jax.ShapeDtypeStruct(shape, BF16)),
        in_specs=[SMEM] + [VMEM] * 5,
        out_specs=(VMEM,) * 2,
        scratch_shapes=[pltpu.VMEM((QUARTER, WIDTH), F32), pltpu.VMEM((2, *shape), F32)],
        compiler_params=PARAMS,
        cost_estimate=cost(40),
    )(at, arrived, *shares)


def core_kernel(keep_ref, given_ref, *out_refs):
    for step, out in enumerate(out_refs):
        out[...] = (keep_ref[step] + given_ref[step].astype(F32)).astype(out.dtype)


def sum_core(keep, given):
    shape = keep.shape[1:]
    return pl.pallas_call(
        core_kernel,
        out_shape=[jax.ShapeDtypeStruct(shape, F32)] + [jax.ShapeDtypeStruct(shape, BF16)] * 3,
        in_specs=[VMEM] * 2,
        out_specs=[VMEM] * 4,
        compiler_params=PARAMS,
    )(keep, given)


def sum_kernel(own_ref, first, second, third, out_ref):
    total = own_ref[...]
    for ref in (first, second, third):
        total = total + ref[...].astype(F32)
    out_ref[...] = total.astype(BF16)


def sum_x(own, parts):
    return pl.pallas_call(
        sum_kernel,
        out_shape=jax.ShapeDtypeStruct(own.shape, BF16),
        in_specs=[VMEM] * 4,
        out_specs=VMEM,
        compiler_params=PARAMS,
    )(own, *parts)


def total_kernel(terms_ref, out_ref):
    total = terms_ref[0].astype(F32)
    for c in range(1, 8):
        total = total + terms_ref[c].astype(F32)
    rest = jnp.concatenate(
        [jnp.broadcast_to(total[OWN + a : OWN + a + 1], (8, 128)) for a in range(REST)], axis=0
    )[:OWN]
    line, column = iota((OWN, 128), 0), iota((OWN, 128), 1)
    rest = jnp.where(line % 8 == column // 16, rest, 0.0)
    for shift in (64, 32, 16):
        rest = rest + pltpu.roll(rest, shift, 1)
    out_ref[:, :128] = total[:OWN]
    out_ref[:, 128:] = rest[:, : SHARD - 128]


def add_up(terms):
    return pl.pallas_call(
        total_kernel,
        out_shape=jax.ShapeDtypeStruct((OWN, SHARD), F32),
        in_specs=[VMEM],
        out_specs=VMEM,
        compiler_params=PARAMS,
    )(terms)


def context_kernel(at_ref, table_ref, landed_ref, *refs):
    pieces, outs, (stream_out, weight, sem) = refs[:10], refs[10:13], refs[13:]
    x, core = at_ref[0], at_ref[1]
    copies = []
    for m in range(3):
        for k, ref in enumerate(pieces):
            of_core = core if k < 5 else 1 - core
            of_x = lax.rem(x + (0, 3, 1, 2, 2)[k % 5], 4)
            start = CUT if k % 5 == 4 else 0
            stop = CUT if k % 5 == 3 else 3 * SHARD
            low, high = max(start, m * SHARD), min(stop, (m + 1) * SHARD)
            if low < high:
                base = pl.multiple_of((2 * of_x + of_core) * SHARD + low - m * SHARD, 16)
                from_ref = ref.at[pl.ds(low - start, high - low)]
                to_ref = weight.at[m, pl.ds(base, high - low)]
                copies.append((m, pltpu.make_async_copy(from_ref, to_ref, sem.at[m])))
    for m, copy in copies:
        if m == 0:
            copy.start()
    landed = landed_ref[...].astype(F32).reshape(8 * SLOTS, ROWS_HALF).astype(BF16)
    placed = matmul_tn(table_ref[...], landed).astype(BF16)
    half = MERGE * SLOTS
    placed = jnp.concatenate([placed[:half], placed[half:, : 3 * WIDTH - ROWS_HALF]], axis=1)
    for m, copy in copies:
        if m > 0:
            copy.start()
    stream_out[...] = placed[:, :WIDTH]
    for m, out in enumerate(outs):
        for of_m, copy in copies:
            if of_m == m:
                copy.wait()
        out[...] = lax.dot_general(
            placed[:, m * WIDTH : (m + 1) * WIDTH],
            weight[m],
            (((1,), (1,)), ((), ())),
            preferred_element_type=F32,
        ).astype(BF16)


def contexts(at, table, landed, pieces):
    out = jax.ShapeDtypeStruct((MERGE * SLOTS, WIDTH), BF16)
    return pl.pallas_call(
        context_kernel,
        out_shape=(out,) * 4,
        in_specs=[SMEM, VMEM, VMEM] + [HBM] * 10,
        out_specs=(VMEM,) * 4,
        scratch_shapes=[
            pltpu.VMEM((3, WIDTH, WIDTH), BF16),
            pltpu.SemaphoreType.DMA((3,)),
        ],
        compiler_params=pltpu.CompilerParams(vmem_limit_bytes=32 << 20),
        cost_estimate=cost(24),
    )(at, table, landed, *pieces)


def local(
    injected_early,
    injected_middle,
    injected_late,
    slot_source,
    saved_early,
    projection_early,
    projection_middle,
    projection_late,
):
    at = jnp.stack([lax.axis_index(name) for name in ("x", "core", "y")]).astype(jnp.int32)

    projections = (projection_early, projection_middle, projection_late)
    message, table = first(slot_source, saved_early[0])
    message, projections = lax.optimization_barrier((message, projections))
    stacked = stack(projections)
    arrived = lax.all_to_all(message, CTX, 0, 0, tiled=True)

    from_left, from_right = over_x(stacked, 1), over_x(stacked, 3)
    injected = injected_early[0], injected_middle[0], injected_late[0]
    share = from_injected(share_kernel, injected, (MERGE * TOKENS, WIDTH), WIDTH)
    rows = from_injected(rows_kernel, injected, (128, 2 * ROWS_HALF), 3 * WIDTH)
    shares = [share] + [over_y(share, step) for step in (1, 2, 3)]
    once_more = from_left[:CUT], from_right[CUT:]
    arrived, shares = lax.optimization_barrier((arrived, shares))

    landed = lax.all_to_all(pack(at, arrived, rows), CTX, 0, 0, tiled=True)

    arrived, shares, from_left, from_right, once_more = lax.optimization_barrier(
        (arrived, shares, from_left, from_right, once_more)
    )
    far = over_x(once_more[0], 1), over_x(once_more[1], 3)
    keep, give = gradient(at, arrived, shares)
    mine, *parts = sum_core(keep, over_core(give))
    parts = [over_x(part, step) for step, part in zip((1, 2, 3), parts)]
    parts, far = lax.optimization_barrier((parts, far))
    terms = sum_x(mine, parts)

    pieces = (stacked, from_left, from_right, *far)
    terms, pieces = lax.optimization_barrier((terms, pieces))
    pieces = pieces + tuple(over_core(piece) for piece in pieces)
    terms, landed = lax.optimization_barrier((terms, landed))
    weights = add_up(lax.all_to_all(terms, "z", 0, 0, tiled=True))
    context_early, context_middle, context_late, stream = contexts(at, table, landed, pieces)
    return context_early[None], context_middle[None], context_late[None], stream[None], weights


def solution(mesh):
    fine = Mesh(mesh.devices.reshape(4, 2, 8, 4), ("x", "core", "z", "y"))
    rows = P(DP, CTX, None)
    return jax.shard_map(
        local,
        mesh=fine,
        in_specs=(rows, rows, rows, P(DP, CTX), rows, P(DP, None), P(DP, None), P(DP, None)),
        out_specs=(rows, rows, rows, rows, P(CTX, DP)),
        check_vma=False,
    )
```

```python
import jax
import jax.numpy as jnp
from jax import lax
from jax.experimental import pallas as pl
from jax.experimental.pallas import tpu as pltpu
from jax.sharding import Mesh, PartitionSpec as P

DP = ("x", "core")
CTX = ("z", "y")
BF16 = jnp.bfloat16
F32 = jnp.float32
VMEM = pl.BlockSpec(memory_space=pltpu.VMEM)
SMEM = pl.BlockSpec(memory_space=pltpu.SMEM)
HBM = pl.BlockSpec(memory_space=pltpu.HBM)
PARAMS = pltpu.CompilerParams(vmem_limit_bytes=16 << 20)


def cost(mib):
    return pl.CostEstimate(flops=0, bytes_accessed=mib << 20, transcendentals=0)


WIDTH = 1152
MERGE = 4
TOKENS = 20
SLOTS = 32
SHARD = 144
CUT = 224
OWN = 36
QUARTER = 288
SAVED_WIDE = 384
SAVED_ROWS = 16
FIRST = 32
ROWS_HALF = 1792
TERM_ROWS = 48
REST = 5


def over_x(array, step):
    return lax.ppermute(array, "x", [(i, (i + step) % 4) for i in range(4)])


def over_y(array, step):
    return lax.ppermute(array, "y", [(i, (i + step) % 4) for i in range(4)])


def over_core(array):
    return lax.ppermute(array, "core", [(0, 1), (1, 0)])


def iota(shape, dim):
    return lax.broadcasted_iota(jnp.int32, shape, dim)


def onehot(condition):
    return jnp.where(condition, 1.0, 0.0).astype(BF16)


def matmul(a, b):
    return jnp.dot(a, b, preferred_element_type=F32)


def matmul_tn(a, b):
    return lax.dot_general(a, b, (((0,), (0,)), ((), ())), preferred_element_type=F32)


def quotient(value, by):
    return jnp.floor((value + 0.5) * (1.0 / by))


def patch_slots(slot):
    source = slot.astype(F32)
    sender = quotient(source, TOKENS)
    place = source - TOKENS * sender
    both = jnp.where(iota((8, SLOTS), 0) == 0, sender, place).astype(BF16)
    repeat = onehot(iota((SLOTS, SLOTS * MERGE), 1) // MERGE == iota((SLOTS, SLOTS * MERGE), 0))
    wide = matmul(both, repeat)
    return wide[0:1], wide[1:2]


def table_kernel(slot_ref, table_ref):
    sender, _ = patch_slots(slot_ref[...])
    count = MERGE * SLOTS
    row, column = iota((2 * count, count), 0), iota((2 * count, count), 1)
    match = (sender == (row // 8).astype(F32)) & (row % MERGE == column % MERGE)
    table_ref[:, :count] = onehot(match & (row % 8 < MERGE))
    table_ref[:, count:] = onehot(match & (row % 8 >= MERGE))


def make_table(slot):
    return pl.pallas_call(
        table_kernel,
        out_shape=jax.ShapeDtypeStruct((8 * SLOTS, 2 * MERGE * SLOTS), BF16),
        in_specs=[VMEM],
        out_specs=VMEM,
        compiler_params=PARAMS,
        cost_estimate=cost(4),
    )(slot)


def first_kernel(slot_hbm, saved_hbm, message_ref, slot_ref, saved_ref, sem):
    fetch_slot = pltpu.make_async_copy(slot_hbm, slot_ref, sem.at[0])
    fetch_saved = pltpu.make_async_copy(saved_hbm, saved_ref, sem.at[1])
    fetch_slot.start()
    fetch_saved.start()
    fetch_slot.wait()

    sender, place = patch_slots(slot_ref[...])
    count = MERGE * SLOTS
    row, column = iota((count, count), 0), iota((count, count), 1)
    match = (sender == (row // MERGE).astype(F32)) & (row % MERGE == column % MERGE)
    tag = jnp.sum(jnp.where(match, place + 1.0, 0.0), axis=1, keepdims=True)
    tag = jnp.broadcast_to(tag, (count, SAVED_WIDE - QUARTER))
    match = onehot(match)
    fetch_saved.wait()
    sorted_rows = matmul(match, saved_ref[...])
    for y in range(4):
        blocks = [sorted_rows[:, OWN * c : OWN * (c + 1)] for c in range(y, SLOTS, 4)]
        message = jnp.concatenate(blocks + [tag], axis=1).astype(BF16)
        for z in range(8):
            message_ref[4 * z + y] = message[SAVED_ROWS * z : SAVED_ROWS * (z + 1)]


def first(slot, saved):
    return pl.pallas_call(
        first_kernel,
        out_shape=jax.ShapeDtypeStruct((SLOTS, SAVED_ROWS, SAVED_WIDE), BF16),
        in_specs=[HBM] * 2,
        out_specs=VMEM,
        scratch_shapes=[
            pltpu.VMEM(slot.shape, jnp.int32),
            pltpu.VMEM(saved.shape, BF16),
            pltpu.SemaphoreType.DMA((2,)),
        ],
        compiler_params=pltpu.CompilerParams(vmem_limit_bytes=58 << 20),
        cost_estimate=cost(8),
    )(slot, saved)


def stack_kernel(early_ref, middle_ref, late_ref, stacked_ref):
    for m, ref in enumerate((early_ref, middle_ref, late_ref)):
        stacked_ref[m * SHARD : (m + 1) * SHARD] = ref[...]


def stack(projections):
    return pl.pallas_call(
        stack_kernel,
        out_shape=jax.ShapeDtypeStruct((3 * SHARD, WIDTH), BF16),
        in_specs=[VMEM] * 3,
        out_specs=VMEM,
        compiler_params=pltpu.CompilerParams(vmem_limit_bytes=8 << 20),
        cost_estimate=cost(4),
    )(*projections)


def add_down(refs, sums, at):
    early_ref, middle_ref, late_ref = refs
    for j in range(MERGE):
        columns = slice(j * WIDTH, (j + 1) * WIDTH)
        to = slice(j * TOKENS, (j + 1) * TOKENS)
        late = late_ref[:, columns].astype(F32)
        middle = late + middle_ref[:, columns].astype(F32)
        sums[to, :WIDTH] = middle + early_ref[:, columns].astype(F32)
        if at > WIDTH:
            sums[to, 2 * WIDTH :] = late
            sums[to, WIDTH : 2 * WIDTH] = middle


def share_kernel(early_ref, middle_ref, late_ref, shares_ref, sums):
    add_down((early_ref, middle_ref, late_ref), sums, WIDTH)
    early = sums[...]
    main = [early[:, d * SHARD : d * SHARD + 128] for d in range(8)]
    rest = [early[:, d * SHARD + 128 : (d + 1) * SHARD] for d in range(8)]
    shares_ref[...] = jnp.concatenate(main + rest, axis=1).astype(BF16)


def rows_kernel(early_ref, middle_ref, late_ref, rows_ref, sums):
    used = MERGE * TOKENS
    add_down((early_ref, middle_ref, late_ref), sums, 3 * WIDTH)
    rows_ref[...] = jnp.zeros_like(rows_ref)
    rows_ref[FIRST : FIRST + used, : 3 * WIDTH] = sums[...].astype(BF16)


def from_injected(kernel, injected, shape, width):
    return pl.pallas_call(
        kernel,
        out_shape=jax.ShapeDtypeStruct(shape, BF16),
        in_specs=[VMEM] * 3,
        out_specs=VMEM,
        scratch_shapes=[pltpu.VMEM((MERGE * TOKENS, width), F32)],
        compiler_params=PARAMS,
        cost_estimate=cost(4),
    )(*injected)


def place_key(column):
    j = sum((column >= k * TOKENS).astype(jnp.int32) for k in range(1, MERGE))
    return column - TOKENS * j + 1 + 32 * j


def pack_kernel(at_ref, arrived_ref, rows_ref, packed_ref):
    arrived = arrived_ref[...].astype(F32).reshape(SLOTS * SAVED_ROWS, SAVED_WIDE).astype(BF16)
    count = MERGE * SLOTS
    shape = (count, SLOTS * SAVED_ROWS)
    row, column = iota(shape, 0), iota(shape, 1)
    mine = MERGE * at_ref[2]
    spread = onehot((row // MERGE == column // SAVED_ROWS) & (column % SAVED_ROWS == mine))
    asked = matmul(spread, arrived[:, SAVED_WIDE - 128 :])
    row, column = iota((count, 128), 0), iota((count, 128), 1)
    inside = (column >= FIRST) & (column < FIRST + MERGE * TOKENS)
    key = place_key(column - FIRST).astype(F32)
    match = onehot(inside & (asked + (32 * (row % MERGE)).astype(F32) == key))
    upper = iota((count, ROWS_HALF), 0) % 8 < MERGE
    left = matmul(match, rows_ref[:, :ROWS_HALF])
    right = matmul(match, rows_ref[:, ROWS_HALF:])
    even = jnp.where(upper, left, pltpu.roll(right, MERGE, 0)).astype(BF16)
    odd = jnp.where(upper, pltpu.roll(left, count - MERGE, 0), right).astype(BF16)
    for k in range(SLOTS // 2):
        packed_ref[2 * k] = even[8 * k : 8 * (k + 1)]
        packed_ref[2 * k + 1] = odd[8 * k : 8 * (k + 1)]


def pack(at, arrived, rows):
    return pl.pallas_call(
        pack_kernel,
        out_shape=jax.ShapeDtypeStruct((SLOTS, 8, ROWS_HALF), BF16),
        in_specs=[SMEM, VMEM, VMEM],
        out_specs=VMEM,
        compiler_params=PARAMS,
        cost_estimate=cost(40),
    )(at, arrived, rows)


def gradient_kernel(at_ref, arrived_ref, *refs):
    shares, (keep_ref, give_ref, product, terms) = refs[:4], refs[4:]
    x, core, y = at_ref[0], at_ref[1], at_ref[2]
    used = MERGE * TOKENS
    arrived = arrived_ref[...].astype(F32).reshape(SLOTS * SAVED_ROWS, SAVED_WIDE)
    row = iota((SLOTS * SAVED_ROWS, 128), 0)
    behind = (y + 4 - row // MERGE % 4) % 4
    tag = arrived[:, SAVED_WIDE - 128 :] + (32 * (row % MERGE) + 128 * behind).astype(F32)
    column = iota((1, 4 * used), 1)
    block = sum((column >= k * used).astype(jnp.int32) for k in range(1, 4))
    key = (place_key(column - used * block) + 128 * block).astype(F32)
    match = onehot(tag[:, 127:128] == key)
    saved = matmul_tn(arrived.astype(BF16), match)[:QUARTER].astype(BF16)
    product[...] = matmul(saved, jnp.concatenate([ref[...] for ref in shares], axis=0))

    line = iota((1, QUARTER), 1).astype(F32)
    block = quotient(line, OWN)
    inside = line - OWN * block
    group = quotient(inside, 8)
    to = 8 * REST * (inside - 8 * group) + REST * block + group
    order = onehot(iota((8 * 8 * REST, QUARTER), 0).astype(F32) == to)
    rest = matmul(order, product[:, 8 * 128 :].astype(BF16))
    at = iota((8 * REST, 128), 1) // 16
    fill = jnp.zeros((TERM_ROWS - OWN - REST, 128), F32)
    for d in range(8):
        folded = jnp.zeros((8 * REST, 128), F32)
        for b in range(8):
            part = rest[8 * REST * b : 8 * REST * (b + 1)]
            if b != d:
                part = pltpu.roll(part, 16 * (b - d) % 128, 1)
            folded = jnp.where(at == b, part, folded)
        step = lax.rem(d // 2 + 4 - x, 4)
        side = lax.rem(d % 2 + core, 2)
        for z in range(8):
            main = product[OWN * z : OWN * (z + 1), 128 * d : 128 * (d + 1)]
            parts = [main, folded[REST * z : REST * (z + 1)], fill]
            terms[side, step, z] = jnp.concatenate(parts, axis=0)
    keep_ref[...] = terms[0]
    give_ref[...] = terms[1].astype(BF16)


def gradient(at, arrived, shares):
    shape = (4, 8, TERM_ROWS, 128)
    return pl.pallas_call(
        gradient_kernel,
        out_shape=(jax.ShapeDtypeStruct(shape, F32), jax.ShapeDtypeStruct(shape, BF16)),
        in_specs=[SMEM] + [VMEM] * 5,
        out_specs=(VMEM,) * 2,
        scratch_shapes=[pltpu.VMEM((QUARTER, WIDTH), F32), pltpu.VMEM((2, *shape), F32)],
        compiler_params=PARAMS,
        cost_estimate=cost(40),
    )(at, arrived, *shares)


def core_kernel(keep_ref, given_ref, *out_refs):
    for step, out in enumerate(out_refs):
        out[...] = (keep_ref[step] + given_ref[step].astype(F32)).astype(out.dtype)


def sum_core(keep, given):
    shape = keep.shape[1:]
    return pl.pallas_call(
        core_kernel,
        out_shape=[jax.ShapeDtypeStruct(shape, F32)] + [jax.ShapeDtypeStruct(shape, BF16)] * 3,
        in_specs=[VMEM] * 2,
        out_specs=[VMEM] * 4,
        compiler_params=PARAMS,
    )(keep, given)


def sum_kernel(own_ref, first, second, third, out_ref):
    total = own_ref[...]
    for ref in (first, second, third):
        total = total + ref[...].astype(F32)
    out_ref[...] = total.astype(BF16)


def sum_x(own, parts):
    return pl.pallas_call(
        sum_kernel,
        out_shape=jax.ShapeDtypeStruct(own.shape, BF16),
        in_specs=[VMEM] * 4,
        out_specs=VMEM,
        compiler_params=PARAMS,
    )(own, *parts)


def total_kernel(terms_ref, out_ref):
    total = terms_ref[0].astype(F32)
    for c in range(1, 8):
        total = total + terms_ref[c].astype(F32)
    rest = jnp.concatenate(
        [jnp.broadcast_to(total[OWN + a : OWN + a + 1], (8, 128)) for a in range(REST)], axis=0
    )[:OWN]
    line, column = iota((OWN, 128), 0), iota((OWN, 128), 1)
    rest = jnp.where(line % 8 == column // 16, rest, 0.0)
    for shift in (64, 32, 16):
        rest = rest + pltpu.roll(rest, shift, 1)
    out_ref[:, :128] = total[:OWN]
    out_ref[:, 128:] = rest[:, : SHARD - 128]


def add_up(terms):
    return pl.pallas_call(
        total_kernel,
        out_shape=jax.ShapeDtypeStruct((OWN, SHARD), F32),
        in_specs=[VMEM],
        out_specs=VMEM,
        compiler_params=PARAMS,
    )(terms)


def context_kernel(at_ref, table_ref, landed_ref, *refs):
    pieces, outs, (stream_out, weight, sem) = refs[:10], refs[10:13], refs[13:]
    x, core = at_ref[0], at_ref[1]
    copies = []
    for m in range(3):
        for k, ref in enumerate(pieces):
            of_core = core if k < 5 else 1 - core
            of_x = lax.rem(x + (0, 3, 1, 2, 2)[k % 5], 4)
            start = CUT if k % 5 == 4 else 0
            stop = CUT if k % 5 == 3 else 3 * SHARD
            low, high = max(start, m * SHARD), min(stop, (m + 1) * SHARD)
            if low < high:
                base = pl.multiple_of((2 * of_x + of_core) * SHARD + low - m * SHARD, 16)
                from_ref = ref.at[pl.ds(low - start, high - low)]
                to_ref = weight.at[m, pl.ds(base, high - low)]
                copies.append((m, pltpu.make_async_copy(from_ref, to_ref, sem.at[m])))
    for m, copy in copies:
        if m == 0:
            copy.start()
    landed = landed_ref[...].astype(F32).reshape(8 * SLOTS, ROWS_HALF).astype(BF16)
    placed = matmul_tn(table_ref[...], landed).astype(BF16)
    half = MERGE * SLOTS
    placed = jnp.concatenate([placed[:half], placed[half:, : 3 * WIDTH - ROWS_HALF]], axis=1)
    for m, copy in copies:
        if m > 0:
            copy.start()
    stream_out[...] = placed[:, :WIDTH]
    for m, out in enumerate(outs):
        for of_m, copy in copies:
            if of_m == m:
                copy.wait()
        out[...] = lax.dot_general(
            placed[:, m * WIDTH : (m + 1) * WIDTH],
            weight[m],
            (((1,), (1,)), ((), ())),
            preferred_element_type=F32,
        ).astype(BF16)


def contexts(at, table, landed, pieces):
    out = jax.ShapeDtypeStruct((MERGE * SLOTS, WIDTH), BF16)
    return pl.pallas_call(
        context_kernel,
        out_shape=(out,) * 4,
        in_specs=[SMEM, VMEM, VMEM] + [HBM] * 10,
        out_specs=(VMEM,) * 4,
        scratch_shapes=[
            pltpu.VMEM((3, WIDTH, WIDTH), BF16),
            pltpu.SemaphoreType.DMA((3,)),
        ],
        compiler_params=pltpu.CompilerParams(vmem_limit_bytes=32 << 20),
        cost_estimate=cost(24),
    )(at, table, landed, *pieces)


def local(
    injected_early,
    injected_middle,
    injected_late,
    slot_source,
    saved_early,
    projection_early,
    projection_middle,
    projection_late,
):
    at = jnp.stack([lax.axis_index(name) for name in ("x", "core", "y")]).astype(jnp.int32)

    projections = (projection_early, projection_middle, projection_late)
    message = first(slot_source, saved_early[0])
    message, projections, slot_source = lax.optimization_barrier(
        (message, projections, slot_source)
    )
    table = make_table(slot_source)
    stacked = stack(projections)
    arrived = lax.all_to_all(message, CTX, 0, 0, tiled=True)

    from_left, from_right = over_x(stacked, 1), over_x(stacked, 3)
    injected = injected_early[0], injected_middle[0], injected_late[0]
    share = from_injected(share_kernel, injected, (MERGE * TOKENS, WIDTH), WIDTH)
    rows = from_injected(rows_kernel, injected, (128, 2 * ROWS_HALF), 3 * WIDTH)
    shares = [share] + [over_y(share, step) for step in (1, 2, 3)]
    once_more = from_left[:CUT], from_right[CUT:]
    arrived, shares = lax.optimization_barrier((arrived, shares))

    landed = lax.all_to_all(pack(at, arrived, rows), CTX, 0, 0, tiled=True)

    arrived, shares, from_left, from_right, once_more = lax.optimization_barrier(
        (arrived, shares, from_left, from_right, once_more)
    )
    far = over_x(once_more[0], 1), over_x(once_more[1], 3)
    keep, give = gradient(at, arrived, shares)
    mine, *parts = sum_core(keep, over_core(give))
    parts = [over_x(part, step) for step, part in zip((1, 2, 3), parts)]
    parts, far = lax.optimization_barrier((parts, far))
    terms = sum_x(mine, parts)

    pieces = (stacked, from_left, from_right, *far)
    terms, pieces = lax.optimization_barrier((terms, pieces))
    pieces = pieces + tuple(over_core(piece) for piece in pieces)
    terms, landed = lax.optimization_barrier((terms, landed))
    weights = add_up(lax.all_to_all(terms, "z", 0, 0, tiled=True))
    context_early, context_middle, context_late, stream = contexts(at, table, landed, pieces)
    return context_early[None], context_middle[None], context_late[None], stream[None], weights


def solution(mesh):
    fine = Mesh(mesh.devices.reshape(4, 2, 8, 4), ("x", "core", "z", "y"))
    rows = P(DP, CTX, None)
    return jax.shard_map(
        local,
        mesh=fine,
        in_specs=(rows, rows, rows, P(DP, CTX), rows, P(DP, None), P(DP, None), P(DP, None)),
        out_specs=(rows, rows, rows, rows, P(CTX, DP)),
        check_vma=False,
    )
```

```python
import jax
import jax.numpy as jnp
from jax import lax
from jax.experimental import pallas as pl
from jax.experimental.pallas import tpu as pltpu
from jax.sharding import Mesh, PartitionSpec as P

DP = ("x", "core")
CTX = ("z", "y")
BF16 = jnp.bfloat16
F32 = jnp.float32
VMEM = pl.BlockSpec(memory_space=pltpu.VMEM)
SMEM = pl.BlockSpec(memory_space=pltpu.SMEM)
HBM = pl.BlockSpec(memory_space=pltpu.HBM)
PARAMS = pltpu.CompilerParams(vmem_limit_bytes=16 << 20)


def cost(mib):
    return pl.CostEstimate(flops=0, bytes_accessed=mib << 20, transcendentals=0)


WIDTH = 1152
MERGE = 4
TOKENS = 20
SLOTS = 32
SHARD = 144
CUT = 224
OWN = 36
QUARTER = 288
SAVED_WIDE = 384
SAVED_ROWS = 16
FIRST = 32
ROWS_HALF = 1792
TERM_ROWS = 48
REST = 5


def over_x(array, step):
    return lax.ppermute(array, "x", [(i, (i + step) % 4) for i in range(4)])


def over_y(array, step):
    return lax.ppermute(array, "y", [(i, (i + step) % 4) for i in range(4)])


def over_core(array):
    return lax.ppermute(array, "core", [(0, 1), (1, 0)])


def iota(shape, dim):
    return lax.broadcasted_iota(jnp.int32, shape, dim)


def onehot(condition):
    return jnp.where(condition, 1.0, 0.0).astype(BF16)


def matmul(a, b):
    return jnp.dot(a, b, preferred_element_type=F32)


def matmul_tn(a, b):
    return lax.dot_general(a, b, (((0,), (0,)), ((), ())), preferred_element_type=F32)


def quotient(value, by):
    return jnp.floor((value + 0.5) * (1.0 / by))


def patch_slots(slot):
    source = slot.astype(F32)
    sender = quotient(source, TOKENS)
    place = source - TOKENS * sender
    both = jnp.where(iota((8, SLOTS), 0) == 0, sender, place).astype(BF16)
    repeat = onehot(iota((SLOTS, SLOTS * MERGE), 1) // MERGE == iota((SLOTS, SLOTS * MERGE), 0))
    wide = matmul(both, repeat)
    return wide[0:1], wide[1:2]


def table_kernel(slot_ref, table_ref):
    sender, _ = patch_slots(slot_ref[...])
    count = MERGE * SLOTS
    row, column = iota((2 * count, count), 0), iota((2 * count, count), 1)
    match = (sender == (row // 8).astype(F32)) & (row % MERGE == column % MERGE)
    table_ref[:, :count] = onehot(match & (row % 8 < MERGE))
    table_ref[:, count:] = onehot(match & (row % 8 >= MERGE))


def make_table(slot):
    return pl.pallas_call(
        table_kernel,
        out_shape=jax.ShapeDtypeStruct((8 * SLOTS, 2 * MERGE * SLOTS), BF16),
        in_specs=[VMEM],
        out_specs=VMEM,
        compiler_params=PARAMS,
        cost_estimate=cost(4),
    )(slot)


def first_kernel(slot_hbm, saved_hbm, message_ref, slot_ref, saved_ref, sem):
    fetch_slot = pltpu.make_async_copy(slot_hbm, slot_ref, sem.at[0])
    fetch_saved = pltpu.make_async_copy(saved_hbm, saved_ref, sem.at[1])
    fetch_slot.start()
    fetch_saved.start()
    fetch_slot.wait()

    sender, place = patch_slots(slot_ref[...])
    count = MERGE * SLOTS
    row, column = iota((count, count), 0), iota((count, count), 1)
    match = (sender == (row // MERGE).astype(F32)) & (row % MERGE == column % MERGE)
    tag = jnp.sum(jnp.where(match, place + 1.0, 0.0), axis=1, keepdims=True)
    tag = jnp.broadcast_to(tag, (count, SAVED_WIDE - QUARTER))
    match = onehot(match)
    fetch_saved.wait()
    sorted_rows = matmul(match, saved_ref[...])
    for y in range(4):
        blocks = [sorted_rows[:, OWN * c : OWN * (c + 1)] for c in range(y, SLOTS, 4)]
        message = jnp.concatenate(blocks + [tag], axis=1).astype(BF16)
        for z in range(8):
            message_ref[4 * z + y] = message[SAVED_ROWS * z : SAVED_ROWS * (z + 1)]


def first(slot, saved):
    return pl.pallas_call(
        first_kernel,
        out_shape=jax.ShapeDtypeStruct((SLOTS, SAVED_ROWS, SAVED_WIDE), BF16),
        in_specs=[HBM] * 2,
        out_specs=VMEM,
        scratch_shapes=[
            pltpu.VMEM(slot.shape, jnp.int32),
            pltpu.VMEM(saved.shape, BF16),
            pltpu.SemaphoreType.DMA((2,)),
        ],
        compiler_params=pltpu.CompilerParams(vmem_limit_bytes=58 << 20),
        cost_estimate=cost(8),
    )(slot, saved)


def stack_kernel(early_ref, middle_ref, late_ref, stacked_ref):
    for m, ref in enumerate((early_ref, middle_ref, late_ref)):
        stacked_ref[m * SHARD : (m + 1) * SHARD] = ref[...]


def stack(projections):
    return pl.pallas_call(
        stack_kernel,
        out_shape=jax.ShapeDtypeStruct((3 * SHARD, WIDTH), BF16),
        in_specs=[VMEM] * 3,
        out_specs=VMEM,
        compiler_params=pltpu.CompilerParams(vmem_limit_bytes=8 << 20),
        cost_estimate=cost(4),
    )(*projections)


def add_down(refs, sums, at):
    early_ref, middle_ref, late_ref = refs
    for j in range(MERGE):
        columns = slice(j * WIDTH, (j + 1) * WIDTH)
        to = slice(j * TOKENS, (j + 1) * TOKENS)
        late = late_ref[:, columns].astype(F32)
        middle = late + middle_ref[:, columns].astype(F32)
        sums[to, :WIDTH] = middle + early_ref[:, columns].astype(F32)
        if at > WIDTH:
            sums[to, 2 * WIDTH :] = late
            sums[to, WIDTH : 2 * WIDTH] = middle


def share_kernel(early_ref, middle_ref, late_ref, shares_ref, sums):
    add_down((early_ref, middle_ref, late_ref), sums, WIDTH)
    early = sums[...]
    main = [early[:, d * SHARD : d * SHARD + 128] for d in range(8)]
    rest = [early[:, d * SHARD + 128 : (d + 1) * SHARD] for d in range(8)]
    shares_ref[...] = jnp.concatenate(main + rest, axis=1).astype(BF16)


def rows_kernel(early_ref, middle_ref, late_ref, rows_ref, sums):
    used = MERGE * TOKENS
    add_down((early_ref, middle_ref, late_ref), sums, 3 * WIDTH)
    rows_ref[...] = jnp.zeros_like(rows_ref)
    rows_ref[FIRST : FIRST + used, : 3 * WIDTH] = sums[...].astype(BF16)


def from_injected(kernel, injected, shape, width):
    return pl.pallas_call(
        kernel,
        out_shape=jax.ShapeDtypeStruct(shape, BF16),
        in_specs=[VMEM] * 3,
        out_specs=VMEM,
        scratch_shapes=[pltpu.VMEM((MERGE * TOKENS, width), F32)],
        compiler_params=PARAMS,
        cost_estimate=cost(4),
    )(*injected)


def place_key(column):
    j = sum((column >= k * TOKENS).astype(jnp.int32) for k in range(1, MERGE))
    return column - TOKENS * j + 1 + 32 * j


def pack_kernel(at_ref, arrived_ref, rows_ref, packed_ref):
    arrived = arrived_ref[...].astype(F32).reshape(SLOTS * SAVED_ROWS, SAVED_WIDE).astype(BF16)
    count = MERGE * SLOTS
    shape = (count, SLOTS * SAVED_ROWS)
    row, column = iota(shape, 0), iota(shape, 1)
    mine = MERGE * at_ref[2]
    spread = onehot((row // MERGE == column // SAVED_ROWS) & (column % SAVED_ROWS == mine))
    asked = matmul(spread, arrived[:, SAVED_WIDE - 128 :])
    row, column = iota((count, 128), 0), iota((count, 128), 1)
    inside = (column >= FIRST) & (column < FIRST + MERGE * TOKENS)
    key = place_key(column - FIRST).astype(F32)
    match = onehot(inside & (asked + (32 * (row % MERGE)).astype(F32) == key))
    upper = iota((count, ROWS_HALF), 0) % 8 < MERGE
    left = matmul(match, rows_ref[:, :ROWS_HALF])
    right = matmul(match, rows_ref[:, ROWS_HALF:])
    even = jnp.where(upper, left, pltpu.roll(right, MERGE, 0)).astype(BF16)
    odd = jnp.where(upper, pltpu.roll(left, count - MERGE, 0), right).astype(BF16)
    for k in range(SLOTS // 2):
        packed_ref[2 * k] = even[8 * k : 8 * (k + 1)]
        packed_ref[2 * k + 1] = odd[8 * k : 8 * (k + 1)]


def pack(at, arrived, rows):
    return pl.pallas_call(
        pack_kernel,
        out_shape=jax.ShapeDtypeStruct((SLOTS, 8, ROWS_HALF), BF16),
        in_specs=[SMEM, VMEM, VMEM],
        out_specs=VMEM,
        compiler_params=PARAMS,
        cost_estimate=cost(40),
    )(at, arrived, rows)


def gradient_kernel(at_ref, arrived_ref, *refs):
    shares, (keep_ref, give_ref, product, terms) = refs[:4], refs[4:]
    x, core, y = at_ref[0], at_ref[1], at_ref[2]
    used = MERGE * TOKENS
    arrived = arrived_ref[...].astype(F32).reshape(SLOTS * SAVED_ROWS, SAVED_WIDE)
    row = iota((SLOTS * SAVED_ROWS, 128), 0)
    behind = (y + 4 - row // MERGE % 4) % 4
    tag = arrived[:, SAVED_WIDE - 128 :] + (32 * (row % MERGE) + 128 * behind).astype(F32)
    column = iota((1, 4 * used), 1)
    block = sum((column >= k * used).astype(jnp.int32) for k in range(1, 4))
    key = (place_key(column - used * block) + 128 * block).astype(F32)
    match = onehot(tag[:, 127:128] == key)
    saved = matmul_tn(arrived.astype(BF16), match)[:QUARTER].astype(BF16)
    product[...] = matmul(saved, jnp.concatenate([ref[...] for ref in shares], axis=0))

    line = iota((1, QUARTER), 1).astype(F32)
    block = quotient(line, OWN)
    inside = line - OWN * block
    group = quotient(inside, 8)
    to = 8 * REST * (inside - 8 * group) + REST * block + group
    order = onehot(iota((8 * 8 * REST, QUARTER), 0).astype(F32) == to)
    rest = matmul(order, product[:, 8 * 128 :].astype(BF16))
    at = iota((8 * REST, 128), 1) // 16
    fill = jnp.zeros((TERM_ROWS - OWN - REST, 128), F32)
    for d in range(8):
        folded = jnp.zeros((8 * REST, 128), F32)
        for b in range(8):
            part = rest[8 * REST * b : 8 * REST * (b + 1)]
            if b != d:
                part = pltpu.roll(part, 16 * (b - d) % 128, 1)
            folded = jnp.where(at == b, part, folded)
        step = lax.rem(d // 2 + 4 - x, 4)
        side = lax.rem(d % 2 + core, 2)
        for z in range(8):
            main = product[OWN * z : OWN * (z + 1), 128 * d : 128 * (d + 1)]
            parts = [main, folded[REST * z : REST * (z + 1)], fill]
            terms[side, step, z] = jnp.concatenate(parts, axis=0)
    keep_ref[...] = terms[0]
    give_ref[...] = terms[1].astype(BF16)


def gradient(at, arrived, shares):
    shape = (4, 8, TERM_ROWS, 128)
    return pl.pallas_call(
        gradient_kernel,
        out_shape=(jax.ShapeDtypeStruct(shape, F32), jax.ShapeDtypeStruct(shape, BF16)),
        in_specs=[SMEM] + [VMEM] * 5,
        out_specs=(VMEM,) * 2,
        scratch_shapes=[pltpu.VMEM((QUARTER, WIDTH), F32), pltpu.VMEM((2, *shape), F32)],
        compiler_params=PARAMS,
        cost_estimate=cost(40),
    )(at, arrived, *shares)


def core_kernel(keep_ref, given_ref, *out_refs):
    for step, out in enumerate(out_refs):
        out[...] = (keep_ref[step] + given_ref[step].astype(F32)).astype(out.dtype)


def sum_core(keep, given):
    shape = keep.shape[1:]
    return pl.pallas_call(
        core_kernel,
        out_shape=[jax.ShapeDtypeStruct(shape, F32)] + [jax.ShapeDtypeStruct(shape, BF16)] * 3,
        in_specs=[VMEM] * 2,
        out_specs=[VMEM] * 4,
        compiler_params=PARAMS,
    )(keep, given)


def sum_kernel(own_ref, first, second, third, out_ref):
    total = own_ref[...]
    for ref in (first, second, third):
        total = total + ref[...].astype(F32)
    out_ref[...] = total.astype(BF16)


def sum_x(own, parts):
    return pl.pallas_call(
        sum_kernel,
        out_shape=jax.ShapeDtypeStruct(own.shape, BF16),
        in_specs=[VMEM] * 4,
        out_specs=VMEM,
        compiler_params=PARAMS,
    )(own, *parts)


def total_kernel(terms_ref, out_ref):
    total = terms_ref[0].astype(F32)
    for c in range(1, 8):
        total = total + terms_ref[c].astype(F32)
    rest = jnp.concatenate(
        [jnp.broadcast_to(total[OWN + a : OWN + a + 1], (8, 128)) for a in range(REST)], axis=0
    )[:OWN]
    line, column = iota((OWN, 128), 0), iota((OWN, 128), 1)
    rest = jnp.where(line % 8 == column // 16, rest, 0.0)
    for shift in (64, 32, 16):
        rest = rest + pltpu.roll(rest, shift, 1)
    out_ref[:, :128] = total[:OWN]
    out_ref[:, 128:] = rest[:, : SHARD - 128]


def add_up(terms):
    return pl.pallas_call(
        total_kernel,
        out_shape=jax.ShapeDtypeStruct((OWN, SHARD), F32),
        in_specs=[VMEM],
        out_specs=VMEM,
        compiler_params=PARAMS,
    )(terms)


def context_kernel(at_ref, table_ref, landed_ref, *refs):
    pieces, outs, (stream_out, weight, sem) = refs[:10], refs[10:13], refs[13:]
    x, core = at_ref[0], at_ref[1]
    copies = []
    for m in range(3):
        for k, ref in enumerate(pieces):
            of_core = core if k < 5 else 1 - core
            of_x = lax.rem(x + (0, 3, 1, 2, 2)[k % 5], 4)
            start = CUT if k % 5 == 4 else 0
            stop = CUT if k % 5 == 3 else 3 * SHARD
            low, high = max(start, m * SHARD), min(stop, (m + 1) * SHARD)
            if low < high:
                base = pl.multiple_of((2 * of_x + of_core) * SHARD + low - m * SHARD, 16)
                from_ref = ref.at[pl.ds(low - start, high - low)]
                to_ref = weight.at[m, pl.ds(base, high - low)]
                copies.append((m, pltpu.make_async_copy(from_ref, to_ref, sem.at[m])))
    for m, copy in copies:
        if m == 0:
            copy.start()
    landed = landed_ref[...].astype(F32).reshape(8 * SLOTS, ROWS_HALF).astype(BF16)
    placed = matmul_tn(table_ref[...], landed).astype(BF16)
    half = MERGE * SLOTS
    placed = jnp.concatenate([placed[:half], placed[half:, : 3 * WIDTH - ROWS_HALF]], axis=1)
    for m, copy in copies:
        if m > 0:
            copy.start()
    stream_out[...] = placed[:, :WIDTH]
    for m, out in enumerate(outs):
        for of_m, copy in copies:
            if of_m == m:
                copy.wait()
        out[...] = lax.dot_general(
            placed[:, m * WIDTH : (m + 1) * WIDTH],
            weight[m],
            (((1,), (1,)), ((), ())),
            preferred_element_type=F32,
        ).astype(BF16)


def contexts(at, table, landed, pieces):
    out = jax.ShapeDtypeStruct((MERGE * SLOTS, WIDTH), BF16)
    return pl.pallas_call(
        context_kernel,
        out_shape=(out,) * 4,
        in_specs=[SMEM, VMEM, VMEM] + [HBM] * 10,
        out_specs=(VMEM,) * 4,
        scratch_shapes=[
            pltpu.VMEM((3, WIDTH, WIDTH), BF16),
            pltpu.SemaphoreType.DMA((3,)),
        ],
        compiler_params=pltpu.CompilerParams(vmem_limit_bytes=32 << 20),
        cost_estimate=cost(24),
    )(at, table, landed, *pieces)


def local(
    injected_early,
    injected_middle,
    injected_late,
    slot_source,
    saved_early,
    projection_early,
    projection_middle,
    projection_late,
):
    at = jnp.stack([lax.axis_index(name) for name in ("x", "core", "y")]).astype(jnp.int32)

    projections = (projection_early, projection_middle, projection_late)
    message = first(slot_source, saved_early[0])
    message, projections, slot_source = lax.optimization_barrier(
        (message, projections, slot_source)
    )
    table = make_table(slot_source)
    stacked = stack(projections)
    arrived = lax.all_to_all(message, CTX, 0, 0, tiled=True)

    from_left, from_right = over_x(stacked, 1), over_x(stacked, 3)
    injected = injected_early[0], injected_middle[0], injected_late[0]
    share = from_injected(share_kernel, injected, (MERGE * TOKENS, WIDTH), WIDTH)
    rows = from_injected(rows_kernel, injected, (128, 2 * ROWS_HALF), 3 * WIDTH)
    shares = [share] + [over_y(share, step) for step in (1, 2, 3)]
    once_more = from_left[:CUT], from_right[CUT:]
    arrived, shares = lax.optimization_barrier((arrived, shares))

    landed = lax.all_to_all(pack(at, arrived, rows), CTX, 0, 0, tiled=True)

    arrived, shares, from_left, from_right, once_more = lax.optimization_barrier(
        (arrived, shares, from_left, from_right, once_more)
    )
    far = over_x(once_more[0], 1), over_x(once_more[1], 3)
    keep, give = gradient(at, arrived, shares)
    given, opposite = lax.optimization_barrier((over_core(give), over_core(stacked)))
    mine, *parts = sum_core(keep, given)
    parts = [over_x(part, step) for step, part in zip((1, 2, 3), parts)]
    parts, far = lax.optimization_barrier((parts, far))
    terms = sum_x(mine, parts)

    pieces = (stacked, from_left, from_right, *far)
    terms, pieces = lax.optimization_barrier((terms, pieces))
    pieces = (*pieces, opposite, *(over_core(piece) for piece in pieces[1:]))
    terms, landed = lax.optimization_barrier((terms, landed))
    weights = add_up(lax.all_to_all(terms, "z", 0, 0, tiled=True))
    context_early, context_middle, context_late, stream = contexts(at, table, landed, pieces)
    return context_early[None], context_middle[None], context_late[None], stream[None], weights


def solution(mesh):
    fine = Mesh(mesh.devices.reshape(4, 2, 8, 4), ("x", "core", "z", "y"))
    rows = P(DP, CTX, None)
    return jax.shard_map(
        local,
        mesh=fine,
        in_specs=(rows, rows, rows, P(DP, CTX), rows, P(DP, None), P(DP, None), P(DP, None)),
        out_specs=(rows, rows, rows, rows, P(CTX, DP)),
        check_vma=False,
    )
```
